512 devices in a mesh: seq: 64 (over y, z_lo, core), head: 8 (over x, z_hi).
Axes of the slice: x: 4, y: 4, z: 16 (z_hi: 2, z_lo: 8; z = z_hi * 8 + z_lo), core: 2. Of those that a mesh axis runs over, the one named last changes fastest.
Arguments:
- query_content: bfloat16 [4096, 64, 128], P('seq', 'head'), may hold values from -15 to 15
- query_rotary: bfloat16 [4096, 4096], P('seq', 'head'), may hold values from -70 to 70
- key_cache: bfloat16 [576, 8192], P(None, 'seq'), may hold values from -5 to 5
- key_up: bfloat16 [512, 64, 128], P(None, 'head'), may hold values from -0.25 to 0.25
- value_up: bfloat16 [512, 64, 128], P(None, 'head'), may hold values from -0.25 to 0.25
- output_weight: bfloat16 [8192, 7168], P('head', 'seq'), may hold values from -0.0625 to 0.0625
- query_start: int32 [1], replicated, may hold values from 3840 to 4096
- key_limit: int32 [1], replicated, may hold values from 7681 to 8192
- block_order: int32 [128], P('seq'), may hold values from 0 to 127, each once
Outputs:
- projected: bfloat16 [4096, 7168], P(('seq', 'head'))
The draws below stay inside these ranges and needn't reach their ends.
Inputs may be any that keep to these rules, and one draw needn't show every extreme that they name: `block_order`: every block number appears in exactly one slot.
All inputs are finite; a program needn't handle non-finite values.
Results may differ from the reference program's by a relative error of at most 0.02.
Values may be sent and summed in bfloat16 or wider, within the bound.
No kernel may reach another device: no remote copies, remote signals or barrier semaphores. Data moves between devices by JAX's collectives and lax.ppermute only.
A program may use at most 64 MiB of HBM per device.

```python
import math
import jax
import jax.numpy as jnp
from jax import lax

WIDTH = 7168
HEADS = 64
NOPE = 128
ROPE = 64
VDIM = 128
LATENT = 512
BLOCK = 32
QUERIES = 4096
KEYS = 8192
N_SEQ = 64


def draw_key_cache(key, part):
    key = jax.random.fold_in(key, 3)
    base = jnp.clip(jax.random.normal(key, (LATENT + ROPE, KEYS), jnp.float32), -5.0, 5.0)
    return base.astype(jnp.bfloat16)


def draw_query_rotary(key, part):
    key = jax.random.fold_in(key, 5)
    base = 2.5 * jnp.clip(jax.random.normal(key, (QUERIES, HEADS * ROPE), jnp.float32), -5.0, 5.0)
    return base.astype(jnp.bfloat16)


def level_of(own_key, dims, pieces, low, largest):
    loudness, own = 1.0, jax.random.fold_in(own_key, 6)
    for dim, blocks in pieces:
        heights = jnp.exp(jax.random.uniform(jax.random.fold_in(own, dim), (blocks,), jnp.float32, low / len(pieces), largest / len(pieces)))
        loudness = loudness * jnp.repeat(heights, dims[dim] // blocks).reshape([-1 if axis == dim else 1 for axis in range(len(dims))])
    return loudness


def noise(stream_key, shape, scale, most, cuts=(), kind=jnp.bfloat16):
    values = jax.random.normal(stream_key, shape, jnp.float32) * scale
    if len(cuts) > 0:
        values = level_of(stream_key, shape, cuts, -0.22, 0.18) * values
    return jnp.clip(values, min=-most, max=most).astype(kind)


def setup_inputs(seed: int = 0) -> dict:
    seeds = jax.random.split(jax.random.key(seed), 10)
    return {
        "query_content": noise(seeds[0], (QUERIES, HEADS, NOPE), 2.5, 15.0, ((0, 64), (1, 8))),
        "query_rotary": draw_query_rotary(jax.random.fold_in(seeds[9], 71), 0),
        "key_cache": draw_key_cache(jax.random.fold_in(seeds[9], 71), 0),
        "key_up": noise(seeds[3], (LATENT, HEADS, NOPE), LATENT ** -0.5, 0.25, ((1, 8),)),
        "value_up": noise(seeds[4], (LATENT, HEADS, VDIM), LATENT ** -0.5, 0.25, ((1, 8),)),
        "output_weight": noise(seeds[5], (HEADS * VDIM, WIDTH), (HEADS * VDIM) ** -0.5, 0.0625, ((0, 8), (1, 64))),
        "query_start": jax.random.randint(seeds[6], (1,), KEYS - QUERIES - QUERIES // 16, KEYS - QUERIES + 1).astype(jnp.int32),
        "key_limit": jax.random.randint(seeds[7], (1,), KEYS - QUERIES // 8 + 1, KEYS + 1).astype(jnp.int32),
        "block_order": jax.random.permutation(seeds[8], 2 * N_SEQ).astype(jnp.int32),
    }


def reference(query_content, query_rotary, key_cache, key_up, value_up, output_weight, query_start, key_limit, block_order):
    token_ids = jnp.arange(QUERIES, dtype=jnp.int32)
    token_positions = query_start[0] + block_order[token_ids // BLOCK] * BLOCK + token_ids % BLOCK
    key_positions = jnp.arange(KEYS, dtype=jnp.int32)
    visible = (key_positions[None, :] <= token_positions[:, None]) & (key_positions[None, :] < key_limit[0])
    latent_query = jnp.einsum('thd,chd->thc', query_content.astype(jnp.float32), key_up.astype(jnp.float32)).astype(jnp.bfloat16)
    rotary = query_rotary.reshape(QUERIES, HEADS, ROPE)
    query_rows = jnp.concatenate([latent_query, rotary], axis=2)
    scale = 1.0 / math.sqrt(NOPE + ROPE)

    def one_head(rows):
        scores = jnp.dot(rows, key_cache, preferred_element_type=jnp.float32) * scale
        scores = jnp.where(visible, scores, -1e+30)
        top = lax.optimization_barrier(jnp.max(scores, axis=1, keepdims=True))
        weights = jnp.where(visible, jnp.exp(scores - top), 0.0)
        total = lax.optimization_barrier(jnp.sum(weights, axis=1, keepdims=True))
        mixed = lax.dot_general(weights.astype(jnp.bfloat16), key_cache[:LATENT], (((1,), (1,)), ((), ())), preferred_element_type=jnp.float32)
        return (mixed / total).astype(jnp.bfloat16)
    mixed_latent = lax.map(one_head, jnp.transpose(query_rows, (1, 0, 2)))
    head_values = jnp.einsum('hqc,chv->qhv', mixed_latent.astype(jnp.float32), value_up.astype(jnp.float32)).astype(jnp.bfloat16)
    flat_values = head_values.reshape(QUERIES, HEADS * VDIM)
    return jnp.dot(flat_values, output_weight, preferred_element_type=jnp.float32).astype(jnp.bfloat16)
```

```python
import functools
import math

import jax
import jax.numpy as jnp
import numpy as np
from jax import lax
from jax.experimental import pallas as pl
from jax.experimental.pallas import tpu as pltpu
from jax.sharding import Mesh, PartitionSpec as P

NEG = -1e30
LOG2E = 1.4426950408889634
SIZES = {"y": 4, "z": 8, "c": 2, "x": 4, "h": 2}
NAMES = tuple(SIZES)
SHIFTS = (1, -1, 2, -2, 3, -3, 4)
STATS = 128


def permute(x, names, move):
    dims = [SIZES[n] for n in names]
    pairs = []
    for place in np.ndindex(*dims):
        target = move(dict(zip(names, place)))
        pairs.append(
            (
                int(np.ravel_multi_index(place, dims)),
                int(np.ravel_multi_index([target[n] for n in names], dims)),
            )
        )
    return lax.ppermute(x, names, pairs)


def along_z(x, step):
    def move(at):
        place = (at["h"] * 8 + at["z"] + step) % 16
        return {"h": place // 8, "z": place % 8}

    return permute(x, ("z", "h"), move)


def other_core(x):
    return permute(x, ("c",), lambda at: {"c": 1 - at["c"]})


def query_kernel(content, rotary, key_up, out):
    head = pl.program_id(0)
    latent = lax.dot_general(
        content[...], key_up[...], (((1,), (1,)), ((), ())), preferred_element_type=jnp.float32
    )
    out[0, :, : latent.shape[1]] = latent.astype(out.dtype)
    pair = rotary[...]
    half = pair.shape[1] // 2
    out[0, :, latent.shape[1] :] = jnp.where(head % 2 == 0, pair[:, :half], pair[:, half:])


def latent_queries(payload, key_up, heads, nope, rope):
    rows = payload.shape[0]
    latent = key_up.shape[0]
    return pl.pallas_call(
        query_kernel,
        grid=(heads,),
        in_specs=[
            pl.BlockSpec((rows, nope), lambda i: (0, i)),
            pl.BlockSpec((rows, 2 * rope), lambda i: (0, heads * nope // (2 * rope) + i // 2)),
            pl.BlockSpec((latent, nope), lambda i: (0, i)),
        ],
        out_specs=pl.BlockSpec((1, rows, latent + rope), lambda i: (i, 0, 0)),
        out_shape=jax.ShapeDtypeStruct((heads, rows, latent + rope), jnp.bfloat16),
    )(payload, payload, key_up)


def attend_kernel(
    starts, bases, limit_ref, query, *rest, shards, coef, latent, block, heads, groups
):
    keys, value_up, out, mixed = rest[:shards], rest[shards], rest[shards + 1], rest[shards + 2]
    group = pl.program_id(0)
    rows = heads * block
    width = keys[0].shape[1]
    limit = limit_ref[0]
    lowest, highest = bases[0], bases[0]
    for i in range(1, shards):
        lowest = jnp.minimum(lowest, bases[i])
        highest = jnp.maximum(highest, bases[i])

    def write(half, normal, lse):
        at = pl.ds(group * 2 * block + half * block, block)
        mixed[:, at, :] = normal.astype(mixed.dtype).reshape(heads, block, latent)
        lane = lax.broadcasted_iota(jnp.int32, (block, STATS), 1)
        parts = []
        left = lse
        for _ in range(3):
            part = left.astype(jnp.bfloat16).astype(jnp.float32)
            parts.append(part)
            left = left - part
        stats = jnp.zeros((block, STATS), jnp.float32)
        for k, part in enumerate(parts):
            for h in range(heads):
                stats = jnp.where(
                    lane == k * heads + h, part[h * block : (h + 1) * block, :], stats
                )
        out[at, out.shape[1] - STATS :] = stats.astype(out.dtype)

    def run(half, masked):
        rows_q = query[:, half * block : (half + 1) * block, :].reshape(rows, -1)
        k = jnp.concatenate([r[...] for r in keys], axis=1)
        s = jnp.dot(rows_q, k, preferred_element_type=jnp.float32)
        if masked:
            token = lax.broadcasted_iota(jnp.int32, (rows, width), 0) % block
            last = jnp.minimum(starts[group * 2 + half] + token, limit - 1)
            lane = lax.broadcasted_iota(jnp.int32, (rows, width), 1)
            s = jnp.concatenate(
                [
                    jnp.where(lane + bases[i] <= last, s[:, i * width : (i + 1) * width], NEG)
                    for i in range(shards)
                ],
                axis=1,
            )
        top = jnp.max(s, axis=1, keepdims=True)
        if masked:
            top = jnp.maximum(top, NEG / 10)
        weights = jnp.exp2(s * coef - top * coef)
        total = jnp.sum(weights, axis=1, keepdims=True)
        values = lax.dot_general(
            weights.astype(jnp.bfloat16),
            k[:latent],
            (((1,), (1,)), ((), ())),
            preferred_element_type=jnp.float32,
        )
        if masked:
            some = total > 0
            safe = jnp.where(some, total, 1.0)
            write(half, values / safe, jnp.where(some, top * coef + jnp.log2(safe), NEG))
        else:
            write(half, values / total, top * coef + jnp.log2(total))

    for half in range(2):
        start = starts[group * 2 + half]
        sure = highest + width - 1 <= jnp.minimum(start, limit - 1)
        some = lowest <= jnp.minimum(start + block - 1, limit - 1)

        @pl.when(sure)
        def _():
            run(half, False)

        @pl.when(jnp.logical_and(some, jnp.logical_not(sure)))
        def _():
            run(half, True)

        @pl.when(jnp.logical_not(some))
        def _():
            write(half, jnp.zeros((rows, latent), jnp.float32), jnp.full((rows, 1), NEG))

    @pl.when(group == groups - 1)
    def _():
        for h in range(heads):
            cols = slice(h * 128, (h + 1) * 128)
            out[:, cols] = jnp.dot(
                mixed[h], value_up[:, cols], preferred_element_type=jnp.float32
            ).astype(out.dtype)


def attend(starts, bases, limit, query, keys, value_up, scale):
    heads, tokens, depth = query.shape
    latent, value_width = value_up.shape
    shards = len(keys)
    groups = starts.shape[0] // 2
    per_group = tokens // groups
    whole = lambda shape: pl.BlockSpec(shape, lambda i, *_: (0, 0))
    kernel = functools.partial(
        attend_kernel,
        shards=shards,
        coef=scale * LOG2E,
        latent=latent,
        block=per_group // 2,
        heads=heads,
        groups=groups,
    )
    return pl.pallas_call(
        kernel,
        grid_spec=pltpu.PrefetchScalarGridSpec(
            num_scalar_prefetch=3,
            grid=(groups,),
            in_specs=[pl.BlockSpec((heads, per_group, depth), lambda i, *_: (0, i, 0))]
            + [whole(k.shape) for k in keys]
            + [whole(value_up.shape)],
            out_specs=whole((tokens, value_width + STATS)),
            scratch_shapes=[pltpu.VMEM((heads, tokens, latent), jnp.bfloat16)],
        ),
        out_shape=jax.ShapeDtypeStruct((tokens, value_width + STATS), jnp.bfloat16),
        compiler_params=pltpu.CompilerParams(vmem_limit_bytes=48 * 1024 * 1024),
    )(starts, bases, limit, query, *keys, value_up)


def merge_kernel(parts, out, *, heads, sources):
    width = out.shape[1]
    each = width // heads
    lses = []
    for s in range(sources):
        stats = parts[s, :, width:].astype(jnp.float32)
        lses.append(
            stats[:, :heads] + stats[:, heads : 2 * heads] + stats[:, 2 * heads : 3 * heads]
        )
    top = functools.reduce(jnp.maximum, lses)
    weights = [jnp.exp2(v - top) for v in lses]
    total = functools.reduce(jnp.add, weights)
    weights = [w / total for w in weights]
    for h in range(heads):
        cols = slice(h * each, (h + 1) * each)
        value = functools.reduce(
            jnp.add,
            [
                weights[s][:, h : h + 1] * parts[s, :, cols].astype(jnp.float32)
                for s in range(sources)
            ],
        )
        out[:, cols] = value.astype(out.dtype)


def merge(parts, heads):
    sources, tokens, width = parts.shape
    return pl.pallas_call(
        functools.partial(merge_kernel, heads=heads, sources=sources),
        out_shape=jax.ShapeDtypeStruct((tokens, width - STATS), jnp.bfloat16),
    )(parts)


def per_device(
    query_content,
    query_rotary,
    key_cache,
    key_up,
    value_up,
    output_weight,
    query_start,
    key_limit,
    block_order,
):
    tokens, heads, nope = query_content.shape
    latent = key_up.shape[0]
    rope = query_rotary.shape[1] // heads
    value_dim = value_up.shape[2]
    columns = output_weight.shape[1]
    block = tokens // 2
    scale = 1.0 / math.sqrt(nope + rope)
    shard = key_cache.shape[1]
    y, z, c = lax.axis_index("y"), lax.axis_index("z"), lax.axis_index("c")

    shards = [key_cache] + [along_z(key_cache, s) for s in SHIFTS]
    offsets = jnp.array((0,) + SHIFTS, jnp.int32)
    bases = ((y * 8 + (z - offsets) % 8) * 2 + c).astype(jnp.int32) * shard

    weight = lax.all_gather(output_weight.T, ("z", "c"), axis=0, tiled=True)

    numbers = jnp.repeat(block_order, block, total_repeat_length=tokens).astype(jnp.bfloat16)
    payload = jnp.concatenate(
        [
            query_content.reshape(tokens, heads * nope),
            query_rotary,
            jnp.broadcast_to(numbers[:, None], (tokens, STATS)),
        ],
        axis=1,
    )
    payload = lax.all_gather(payload, "y", axis=0)
    partner = other_core(payload)
    first = jnp.where(c == 0, payload, partner)
    second = jnp.where(c == 0, partner, payload)
    payload = jnp.stack([first, second], axis=1).reshape(8 * tokens, -1)
    starts = query_start[0] + payload[::block, -1].astype(jnp.int32) * block

    queries = latent_queries(payload, key_up.reshape(latent, heads * nope), heads, nope, rope)
    partial = attend(
        starts,
        bases,
        key_limit,
        queries,
        shards,
        value_up.reshape(latent, heads * value_dim),
        scale,
    )
    partial = lax.all_to_all(
        partial.reshape(8, tokens, -1), ("y", "c"), split_axis=0, concat_axis=0, tiled=True
    )
    values = merge(partial, heads)

    rows = lax.all_gather(values, "y", axis=0, tiled=True)
    product = lax.dot_general(
        rows, weight, (((1,), (1,)), ((), ())), preferred_element_type=jnp.float32
    ).astype(jnp.bfloat16)
    share = tokens // 8
    width = 16 * columns
    product = lax.all_to_all(
        product.reshape(32, share, width), ("y", "x", "h"), split_axis=0, concat_axis=0, tiled=True
    )
    summed = jnp.sum(product.reshape(4, 8, share, width).astype(jnp.float32), axis=1)
    return summed.astype(jnp.bfloat16).transpose(1, 0, 2).reshape(share, 4 * width)


def solution(mesh):
    fine = Mesh(mesh.devices.reshape(tuple(SIZES.values())), NAMES)
    seq, head = ("y", "z", "c"), ("x", "h")
    in_specs = (
        P(seq, head, None),
        P(seq, head),
        P(None, seq),
        P(None, head, None),
        P(None, head, None),
        P(head, seq),
        P(),
        P(),
        P(seq),
    )
    return jax.shard_map(
        per_device, mesh=fine, in_specs=in_specs, out_specs=P(seq + head, None), check_vma=False
    )
```

```python
import functools
import math

import jax
import jax.numpy as jnp
import numpy as np
from jax import lax
from jax.experimental import pallas as pl
from jax.experimental.pallas import tpu as pltpu
from jax.sharding import Mesh, PartitionSpec as P

NEG = -1e30
LOG2E = 1.4426950408889634
SIZES = {"y": 4, "z": 8, "c": 2, "x": 4, "h": 2}
NAMES = tuple(SIZES)
STATS = 128


def permute(x, names, move):
    dims = [SIZES[n] for n in names]
    pairs = []
    for place in np.ndindex(*dims):
        target = move(dict(zip(names, place)))
        pairs.append(
            (
                int(np.ravel_multi_index(place, dims)),
                int(np.ravel_multi_index([target[n] for n in names], dims)),
            )
        )
    return lax.ppermute(x, names, pairs)


def along_z(x, step):
    def move(at):
        place = (at["h"] * 8 + at["z"] + (step if at["c"] == 0 else -step)) % 16
        return {"z": place % 8, "c": at["c"], "h": place // 8}

    return permute(x, ("z", "c", "h"), move)


def other_core(x):
    return permute(x, ("c",), lambda at: {"c": 1 - at["c"]})


def to_all_y(x):
    return lax.all_to_all(
        jnp.broadcast_to(x[None], (4,) + x.shape), "y", split_axis=0, concat_axis=0, tiled=True
    )


def pack_kernel(order, content, rotary, out, *, block):
    left = content.shape[1]
    out[:, :left] = content[...]
    out[:, left : left + rotary.shape[1]] = rotary[...]
    row = lax.broadcasted_iota(jnp.int32, (out.shape[0], STATS), 0)
    number = jnp.where(row < block, order[0], order[1])
    out[:, left + rotary.shape[1] :] = number.astype(jnp.float32).astype(out.dtype)


def pack(order, content, rotary, block):
    rows = content.shape[0]
    width = content.shape[1] + rotary.shape[1] + STATS
    vmem = pl.BlockSpec(memory_space=pltpu.VMEM)
    return pl.pallas_call(
        functools.partial(pack_kernel, block=block),
        in_specs=[pl.BlockSpec(memory_space=pltpu.SMEM), vmem, vmem],
        out_specs=vmem,
        out_shape=jax.ShapeDtypeStruct((rows, width), jnp.bfloat16),
    )(order, content, rotary)


def query_kernel(content, rotary, key_up, out):
    head = pl.program_id(0)
    latent = lax.dot_general(
        content[...], key_up[...], (((1,), (1,)), ((), ())), preferred_element_type=jnp.float32
    )
    out[0, :, : latent.shape[1]] = latent.astype(out.dtype)
    pair = rotary[...]
    half = pair.shape[1] // 2
    out[0, :, latent.shape[1] :] = jnp.where(head % 2 == 0, pair[:, :half], pair[:, half:])


def latent_queries(payload, key_up, heads, nope, rope):
    rows = payload.shape[0]
    latent = key_up.shape[0]
    return pl.pallas_call(
        query_kernel,
        grid=(heads,),
        in_specs=[
            pl.BlockSpec((rows, nope), lambda i: (0, i)),
            pl.BlockSpec((rows, 2 * rope), lambda i: (0, heads * nope // (2 * rope) + i // 2)),
            pl.BlockSpec((latent, nope), lambda i: (0, i)),
        ],
        out_specs=pl.BlockSpec((1, rows, latent + rope), lambda i: (i, 0, 0)),
        out_shape=jax.ShapeDtypeStruct((heads, rows, latent + rope), jnp.bfloat16),
    )(payload, payload, key_up)


def attend_kernel(
    starts, bases, limit_ref, query, *rest, shards, coef, latent, block, heads, groups
):
    *keys, value_up, out, mixed = rest
    group = pl.program_id(0)
    rows = heads * block
    width = keys[0].shape[2]
    limit = limit_ref[0]
    lowest, highest = bases[0], bases[0]
    for i in range(1, shards):
        lowest = jnp.minimum(lowest, bases[i])
        highest = jnp.maximum(highest, bases[i])

    def write(half, normal, lse):
        at = pl.ds(group * 2 * block + half * block, block)
        mixed[:, at, :] = normal.astype(mixed.dtype).reshape(heads, block, latent)
        lane = lax.broadcasted_iota(jnp.int32, (block, STATS), 1)
        parts = []
        left = lse
        for _ in range(3):
            part = left.astype(jnp.bfloat16).astype(jnp.float32)
            parts.append(part)
            left = left - part
        stats = jnp.zeros((block, STATS), jnp.float32)
        for k, part in enumerate(parts):
            for h in range(heads):
                stats = jnp.where(
                    lane == k * heads + h, part[h * block : (h + 1) * block, :], stats
                )
        out[at, out.shape[1] - STATS :] = stats.astype(out.dtype)

    def run(half, masked):
        rows_q = query[:, half * block : (half + 1) * block, :].reshape(rows, -1)
        k = jnp.concatenate([r[i] for r in keys for i in range(r.shape[0])], axis=1)
        s = jnp.dot(rows_q, k, preferred_element_type=jnp.float32)
        if masked:
            token = lax.broadcasted_iota(jnp.int32, (rows, width), 0) % block
            last = jnp.minimum(starts[group * 2 + half] + token, limit - 1)
            lane = lax.broadcasted_iota(jnp.int32, (rows, width), 1)
            s = jnp.concatenate(
                [
                    jnp.where(lane + bases[i] <= last, s[:, i * width : (i + 1) * width], NEG)
                    for i in range(shards)
                ],
                axis=1,
            )
        top = jnp.max(s, axis=1, keepdims=True)
        if masked:
            top = jnp.maximum(top, NEG / 10)
        weights = jnp.exp2(s * coef - top * coef)
        total = jnp.sum(weights, axis=1, keepdims=True)
        values = lax.dot_general(
            weights.astype(jnp.bfloat16),
            k[:latent],
            (((1,), (1,)), ((), ())),
            preferred_element_type=jnp.float32,
        )
        if masked:
            some = total > 0
            safe = jnp.where(some, total, 1.0)
            write(half, values / safe, jnp.where(some, top * coef + jnp.log2(safe), NEG))
        else:
            write(half, values / total, top * coef + jnp.log2(total))

    for half in range(2):
        start = starts[group * 2 + half]
        sure = highest + width - 1 <= jnp.minimum(start, limit - 1)
        some = lowest <= jnp.minimum(start + block - 1, limit - 1)

        @pl.when(sure)
        def _():
            run(half, False)

        @pl.when(jnp.logical_and(some, jnp.logical_not(sure)))
        def _():
            run(half, True)

        @pl.when(jnp.logical_not(some))
        def _():
            write(half, jnp.zeros((rows, latent), jnp.float32), jnp.full((rows, 1), NEG))

    @pl.when(group == groups - 1)
    def _():
        for h in range(heads):
            cols = slice(h * 128, (h + 1) * 128)
            out[:, cols] = jnp.dot(
                mixed[h], value_up[:, cols], preferred_element_type=jnp.float32
            ).astype(out.dtype)


def attend(starts, bases, limit, query, keys, value_up, scale):
    heads, tokens, depth = query.shape
    latent, value_width = value_up.shape
    shards = sum(k.shape[0] for k in keys)
    groups = starts.shape[0] // 2
    per_group = tokens // groups
    whole = lambda shape: pl.BlockSpec(shape, lambda i, *_: (0,) * len(shape))
    kernel = functools.partial(
        attend_kernel,
        shards=shards,
        coef=scale * LOG2E,
        latent=latent,
        block=per_group // 2,
        heads=heads,
        groups=groups,
    )
    return pl.pallas_call(
        kernel,
        grid_spec=pltpu.PrefetchScalarGridSpec(
            num_scalar_prefetch=3,
            grid=(groups,),
            in_specs=[pl.BlockSpec((heads, per_group, depth), lambda i, *_: (0, i, 0))]
            + [whole(k.shape) for k in keys]
            + [whole(value_up.shape)],
            out_specs=whole((tokens, value_width + STATS)),
            scratch_shapes=[pltpu.VMEM((heads, tokens, latent), jnp.bfloat16)],
        ),
        out_shape=jax.ShapeDtypeStruct((tokens, value_width + STATS), jnp.bfloat16),
        compiler_params=pltpu.CompilerParams(vmem_limit_bytes=48 * 1024 * 1024),
    )(starts, bases, limit, query, *keys, value_up)


def merge_kernel(parts, out, *, heads, sources):
    width = out.shape[1]
    each = width // heads
    lses = []
    for s in range(sources):
        stats = parts[s, :, width:].astype(jnp.float32)
        lses.append(
            stats[:, :heads] + stats[:, heads : 2 * heads] + stats[:, 2 * heads : 3 * heads]
        )
    top = functools.reduce(jnp.maximum, lses)
    weights = [jnp.exp2(v - top) for v in lses]
    total = functools.reduce(jnp.add, weights)
    weights = [w / total for w in weights]
    for h in range(heads):
        cols = slice(h * each, (h + 1) * each)
        value = functools.reduce(
            jnp.add,
            [
                weights[s][:, h : h + 1] * parts[s, :, cols].astype(jnp.float32)
                for s in range(sources)
            ],
        )
        out[:, cols] = value.astype(out.dtype)


def merge(parts, heads):
    sources, tokens, width = parts.shape
    return pl.pallas_call(
        functools.partial(merge_kernel, heads=heads, sources=sources),
        out_shape=jax.ShapeDtypeStruct((tokens, width - STATS), jnp.bfloat16),
    )(parts)


def per_device(
    query_content,
    query_rotary,
    key_cache,
    key_up,
    value_up,
    output_weight,
    query_start,
    key_limit,
    block_order,
):
    tokens, heads, nope = query_content.shape
    latent = key_up.shape[0]
    rope = query_rotary.shape[1] // heads
    value_dim = value_up.shape[2]
    columns = output_weight.shape[1]
    block = tokens // 2
    scale = 1.0 / math.sqrt(nope + rope)
    shard = key_cache.shape[1]
    y, z, c, h = (lax.axis_index(n) for n in ("y", "z", "c", "h"))

    pair = jnp.stack([key_cache, other_core(key_cache)])
    fetched = jnp.concatenate(
        [along_z(pair, s) for s in (1, 2, 3)] + [along_z(key_cache, 4)[None]], axis=0
    )
    keys = [pair, fetched, other_core(fetched)]
    side = 1 - 2 * c
    steps = np.array([0, 0, 1, 1, 2, 2, 3, 3, 4, -1, -1, -2, -2, -3, -3, -4], np.int32)
    cores = np.array([0, 1, 0, 1, 0, 1, 0, 1, 0, 1, 0, 1, 0, 1, 0, 1], np.int32)
    bases = ((y * 8 + (z - side * steps) % 8) * 2 + (c + cores) % 2).astype(jnp.int32) * shard

    weight = lax.all_gather(output_weight.T, "z", axis=0, tiled=True)
    weights = [weight, other_core(weight)]

    payload = pack(block_order, query_content.reshape(tokens, heads * nope), query_rotary, block)
    payload = to_all_y(payload).reshape(4 * tokens, -1)
    starts = query_start[0] + payload[::block, -1].astype(jnp.int32) * block

    queries = latent_queries(payload, key_up.reshape(latent, heads * nope), heads, nope, rope)
    partial = attend(
        starts,
        bases,
        key_limit,
        queries,
        keys,
        value_up.reshape(latent, heads * value_dim),
        scale,
    )
    partial = lax.all_to_all(
        partial.reshape(4, tokens, -1), "y", split_axis=0, concat_axis=0, tiled=True
    )
    values = merge(partial, heads)

    rows = to_all_y(values).reshape(4 * tokens, -1)
    product = jnp.concatenate(
        [
            lax.dot_general(
                rows, w, (((1,), (1,)), ((), ())), preferred_element_type=jnp.float32
            ).astype(jnp.bfloat16)
            for w in weights
        ],
        axis=1,
    )
    share = tokens // 8
    width = 16 * columns
    product = lax.all_to_all(
        product.reshape(16, 2 * share, width), ("y", "x"), split_axis=0, concat_axis=0, tiled=True
    )
    summed = jnp.sum(product.reshape(4, 4, 2, share, width).astype(jnp.float32), axis=1)
    mine = jnp.where(h == 0, summed[:, 0], summed[:, 1])
    theirs = jnp.where(h == 0, summed[:, 1], summed[:, 0]).astype(jnp.bfloat16)
    got = permute(theirs, ("h",), lambda at: {"h": 1 - at["h"]})
    total = (mine + got.astype(jnp.float32)).astype(jnp.bfloat16)
    total = total.reshape(4, share, 2, 8, columns)
    total = jnp.where(c == 0, total, total[:, :, ::-1])
    return total.transpose(1, 0, 3, 2, 4).reshape(share, 4 * width)


def solution(mesh):
    fine = Mesh(mesh.devices.reshape(tuple(SIZES.values())), NAMES)
    seq, head = ("y", "z", "c"), ("x", "h")
    in_specs = (
        P(seq, head, None),
        P(seq, head),
        P(None, seq),
        P(None, head, None),
        P(None, head, None),
        P(head, seq),
        P(),
        P(),
        P(seq),
    )
    return jax.shard_map(
        per_device, mesh=fine, in_specs=in_specs, out_specs=P(seq + head, None), check_vma=False
    )
```

```python
import functools
import math

import jax
import jax.numpy as jnp
import numpy as np
from jax import lax
from jax.experimental import pallas as pl
from jax.experimental.pallas import tpu as pltpu
from jax.sharding import Mesh, PartitionSpec as P

NEG = -1e30
LOG2E = 1.4426950408889634
SIZES = {"y": 4, "z": 8, "c": 2, "x": 4, "h": 2}
NAMES = tuple(SIZES)
STATS = 128


def permute(x, names, move):
    dims = [SIZES[n] for n in names]
    pairs = []
    for place in np.ndindex(*dims):
        target = move(dict(zip(names, place)))
        pairs.append(
            (
                int(np.ravel_multi_index(place, dims)),
                int(np.ravel_multi_index([target[n] for n in names], dims)),
            )
        )
    return lax.ppermute(x, names, pairs)


def along_z(x, step):
    def move(at):
        place = (at["h"] * 8 + at["z"] + (step if at["c"] == 0 else -step)) % 16
        return {"z": place % 8, "c": at["c"], "h": place // 8}

    return permute(x, ("z", "c", "h"), move)


def other_core(x):
    return permute(x, ("c",), lambda at: {"c": 1 - at["c"]})


def to_all_y(x):
    return lax.all_to_all(
        jnp.broadcast_to(x[None], (4,) + x.shape), "y", split_axis=0, concat_axis=0, tiled=True
    )


def pack_kernel(order, content, rotary, out, *, block):
    left = content.shape[1]
    out[:, :left] = content[...]
    out[:, left : left + rotary.shape[1]] = rotary[...]
    row = lax.broadcasted_iota(jnp.int32, (out.shape[0], STATS), 0)
    number = jnp.where(row < block, order[0], order[1])
    out[:, left + rotary.shape[1] :] = number.astype(jnp.float32).astype(out.dtype)


def pack(order, content, rotary, block):
    rows = content.shape[0]
    width = content.shape[1] + rotary.shape[1] + STATS
    vmem = pl.BlockSpec(memory_space=pltpu.VMEM)
    return pl.pallas_call(
        functools.partial(pack_kernel, block=block),
        in_specs=[pl.BlockSpec(memory_space=pltpu.SMEM), vmem, vmem],
        out_specs=vmem,
        out_shape=jax.ShapeDtypeStruct((rows, width), jnp.bfloat16),
    )(order, content, rotary)


def query_kernel(content, rotary, key_up, out):
    head = pl.program_id(0)
    latent = lax.dot_general(
        content[...], key_up[...], (((1,), (1,)), ((), ())), preferred_element_type=jnp.float32
    )
    out[0, :, : latent.shape[1]] = latent.astype(out.dtype)
    pair = rotary[...]
    half = pair.shape[1] // 2
    out[0, :, latent.shape[1] :] = jnp.where(head % 2 == 0, pair[:, :half], pair[:, half:])


def latent_queries(payload, key_up, heads, nope, rope):
    rows = payload.shape[0]
    latent = key_up.shape[0]
    return pl.pallas_call(
        query_kernel,
        grid=(heads,),
        in_specs=[
            pl.BlockSpec((rows, nope), lambda i: (0, i)),
            pl.BlockSpec((rows, 2 * rope), lambda i: (0, heads * nope // (2 * rope) + i // 2)),
            pl.BlockSpec((latent, nope), lambda i: (0, i)),
        ],
        out_specs=pl.BlockSpec((1, rows, latent + rope), lambda i: (i, 0, 0)),
        out_shape=jax.ShapeDtypeStruct((heads, rows, latent + rope), jnp.bfloat16),
        cost_estimate=pl.CostEstimate(
            flops=2 * heads * rows * latent * nope, bytes_accessed=8 * 1024 * 1024, transcendentals=0
        ),
    )(payload, payload, key_up)


def attend_kernel(
    starts, bases, limit_ref, query, *rest, shards, coef, latent, block, heads, groups
):
    *keys, value_up, out, mixed = rest
    group = pl.program_id(0)
    rows = heads * block
    width = keys[0].shape[2]
    limit = limit_ref[0]
    lowest, highest = bases[0], bases[0]
    for i in range(1, shards):
        lowest = jnp.minimum(lowest, bases[i])
        highest = jnp.maximum(highest, bases[i])

    def write(half, normal, lse):
        at = pl.ds(group * 2 * block + half * block, block)
        mixed[:, at, :] = normal.astype(mixed.dtype).reshape(heads, block, latent)
        lane = lax.broadcasted_iota(jnp.int32, (block, STATS), 1)
        parts = []
        left = lse
        for _ in range(3):
            part = left.astype(jnp.bfloat16).astype(jnp.float32)
            parts.append(part)
            left = left - part
        stats = jnp.zeros((block, STATS), jnp.float32)
        for k, part in enumerate(parts):
            for h in range(heads):
                stats = jnp.where(
                    lane == k * heads + h, part[h * block : (h + 1) * block, :], stats
                )
        out[at, out.shape[1] - STATS :] = stats.astype(out.dtype)

    def run(half, masked):
        rows_q = query[:, half * block : (half + 1) * block, :].reshape(rows, -1)
        k = jnp.concatenate([r[i] for r in keys for i in range(r.shape[0])], axis=1)
        s = jnp.dot(rows_q, k, preferred_element_type=jnp.float32)
        if masked:
            token = lax.broadcasted_iota(jnp.int32, (rows, width), 0) % block
            last = jnp.minimum(starts[group * 2 + half] + token, limit - 1)
            lane = lax.broadcasted_iota(jnp.int32, (rows, width), 1)
            s = jnp.concatenate(
                [
                    jnp.where(lane + bases[i] <= last, s[:, i * width : (i + 1) * width], NEG)
                    for i in range(shards)
                ],
                axis=1,
            )
        top = jnp.max(s, axis=1, keepdims=True)
        if masked:
            top = jnp.maximum(top, NEG / 10)
        weights = jnp.exp2(s * coef - top * coef)
        total = jnp.sum(weights, axis=1, keepdims=True)
        values = lax.dot_general(
            weights.astype(jnp.bfloat16),
            k[:latent],
            (((1,), (1,)), ((), ())),
            preferred_element_type=jnp.float32,
        )
        if masked:
            some = total > 0
            safe = jnp.where(some, total, 1.0)
            write(half, values / safe, jnp.where(some, top * coef + jnp.log2(safe), NEG))
        else:
            write(half, values / total, top * coef + jnp.log2(total))

    for half in range(2):
        start = starts[group * 2 + half]
        sure = highest + width - 1 <= jnp.minimum(start, limit - 1)
        some = lowest <= jnp.minimum(start + block - 1, limit - 1)

        @pl.when(sure)
        def _():
            run(half, False)

        @pl.when(jnp.logical_and(some, jnp.logical_not(sure)))
        def _():
            run(half, True)

        @pl.when(jnp.logical_not(some))
        def _():
            write(half, jnp.zeros((rows, latent), jnp.float32), jnp.full((rows, 1), NEG))

    @pl.when(group == groups - 1)
    def _():
        for h in range(heads):
            cols = slice(h * 128, (h + 1) * 128)
            out[:, cols] = jnp.dot(
                mixed[h], value_up[:, cols], preferred_element_type=jnp.float32
            ).astype(out.dtype)


def attend(starts, bases, limit, query, keys, value_up, scale):
    heads, tokens, depth = query.shape
    latent, value_width = value_up.shape
    shards = sum(k.shape[0] for k in keys)
    groups = starts.shape[0] // 2
    per_group = tokens // groups
    whole = lambda shape: pl.BlockSpec(shape, lambda i, *_: (0,) * len(shape))
    kernel = functools.partial(
        attend_kernel,
        shards=shards,
        coef=scale * LOG2E,
        latent=latent,
        block=per_group // 2,
        heads=heads,
        groups=groups,
    )
    return pl.pallas_call(
        kernel,
        grid_spec=pltpu.PrefetchScalarGridSpec(
            num_scalar_prefetch=3,
            grid=(groups,),
            in_specs=[pl.BlockSpec((heads, per_group, depth), lambda i, *_: (0, i, 0))]
            + [whole(k.shape) for k in keys]
            + [whole(value_up.shape)],
            out_specs=whole((tokens, value_width + STATS)),
            scratch_shapes=[pltpu.VMEM((heads, tokens, latent), jnp.bfloat16)],
        ),
        out_shape=jax.ShapeDtypeStruct((tokens, value_width + STATS), jnp.bfloat16),
        compiler_params=pltpu.CompilerParams(vmem_limit_bytes=48 * 1024 * 1024),
    )(starts, bases, limit, query, *keys, value_up)


def merge_kernel(parts, out, *, heads, sources):
    width = out.shape[1]
    each = width // heads
    lses = []
    for s in range(sources):
        stats = parts[s, :, width:].astype(jnp.float32)
        lses.append(
            stats[:, :heads] + stats[:, heads : 2 * heads] + stats[:, 2 * heads : 3 * heads]
        )
    top = functools.reduce(jnp.maximum, lses)
    weights = [jnp.exp2(v - top) for v in lses]
    total = functools.reduce(jnp.add, weights)
    weights = [w / total for w in weights]
    for h in range(heads):
        cols = slice(h * each, (h + 1) * each)
        value = functools.reduce(
            jnp.add,
            [
                weights[s][:, h : h + 1] * parts[s, :, cols].astype(jnp.float32)
                for s in range(sources)
            ],
        )
        out[:, cols] = value.astype(out.dtype)


def merge(parts, heads):
    sources, tokens, width = parts.shape
    return pl.pallas_call(
        functools.partial(merge_kernel, heads=heads, sources=sources),
        out_shape=jax.ShapeDtypeStruct((tokens, width - STATS), jnp.bfloat16),
    )(parts)


def per_device(
    query_content,
    query_rotary,
    key_cache,
    key_up,
    value_up,
    output_weight,
    query_start,
    key_limit,
    block_order,
):
    tokens, heads, nope = query_content.shape
    latent = key_up.shape[0]
    rope = query_rotary.shape[1] // heads
    value_dim = value_up.shape[2]
    columns = output_weight.shape[1]
    block = tokens // 2
    scale = 1.0 / math.sqrt(nope + rope)
    shard = key_cache.shape[1]
    y, z, c, h = (lax.axis_index(n) for n in ("y", "z", "c", "h"))

    weight = lax.all_gather(output_weight.T, "z", axis=0, tiled=True)

    payload = pack(block_order, query_content.reshape(tokens, heads * nope), query_rotary, block)

    pair = jnp.stack([key_cache, other_core(key_cache)])
    payload, pair = lax.optimization_barrier((payload, pair))
    one, two = along_z(pair, 1), along_z(pair, 2)
    payload = to_all_y(payload).reshape(4 * tokens, -1)
    starts = query_start[0] + payload[::block, -1].astype(jnp.int32) * block
    queries = latent_queries(payload, key_up.reshape(latent, heads * nope), heads, nope, rope)
    queries, one, two = lax.optimization_barrier((queries, one, two))
    three, four = along_z(two, 1), along_z(two[:1], 2)
    fetched = jnp.concatenate([one, two, three, four], axis=0)
    keys = [pair, fetched, other_core(fetched)]
    side = 1 - 2 * c
    steps = np.array([0, 0, 1, 1, 2, 2, 3, 3, 4, -1, -1, -2, -2, -3, -3, -4], np.int32)
    cores = np.array([0, 1, 0, 1, 0, 1, 0, 1, 0, 1, 0, 1, 0, 1, 0, 1], np.int32)
    bases = ((y * 8 + (z - side * steps) % 8) * 2 + (c + cores) % 2).astype(jnp.int32) * shard

    partial = attend(
        starts,
        bases,
        key_limit,
        queries,
        keys,
        value_up.reshape(latent, heads * value_dim),
        scale,
    )
    partial = lax.all_to_all(
        partial.reshape(4, tokens, -1), "y", split_axis=0, concat_axis=0, tiled=True
    )
    values = merge(partial, heads)
    values, weight = lax.optimization_barrier((values, weight))
    weights = [weight, other_core(weight)]

    rows = to_all_y(values).reshape(4 * tokens, -1)
    product = jnp.concatenate(
        [
            lax.dot_general(
                rows, w, (((1,), (1,)), ((), ())), preferred_element_type=jnp.float32
            ).astype(jnp.bfloat16)
            for w in weights
        ],
        axis=1,
    )
    share = tokens // 8
    width = 16 * columns
    product = lax.all_to_all(
        product.reshape(16, 2 * share, width), ("y", "x"), split_axis=0, concat_axis=0, tiled=True
    )
    summed = jnp.sum(product.reshape(4, 4, 2, share, width).astype(jnp.float32), axis=1)
    mine = jnp.where(h == 0, summed[:, 0], summed[:, 1])
    theirs = jnp.where(h == 0, summed[:, 1], summed[:, 0]).astype(jnp.bfloat16)
    got = permute(theirs, ("h",), lambda at: {"h": 1 - at["h"]})
    total = (mine + got.astype(jnp.float32)).astype(jnp.bfloat16)
    total = total.reshape(4, share, 2, 8, columns)
    total = jnp.where(c == 0, total, total[:, :, ::-1])
    return total.transpose(1, 0, 3, 2, 4).reshape(share, 4 * width)


def solution(mesh):
    fine = Mesh(mesh.devices.reshape(tuple(SIZES.values())), NAMES)
    seq, head = ("y", "z", "c"), ("x", "h")
    in_specs = (
        P(seq, head, None),
        P(seq, head),
        P(None, seq),
        P(None, head, None),
        P(None, head, None),
        P(head, seq),
        P(),
        P(),
        P(seq),
    )
    return jax.shard_map(
        per_device, mesh=fine, in_specs=in_specs, out_specs=P(seq + head, None), check_vma=False
    )
```

```python
import functools
import math

import jax
import jax.numpy as jnp
import numpy as np
from jax import lax
from jax.experimental import pallas as pl
from jax.experimental.pallas import tpu as pltpu
from jax.sharding import Mesh, PartitionSpec as P

NEG = -1e30
LOG2E = 1.4426950408889634
SIZES = {"y": 4, "z": 8, "c": 2, "x": 4, "h": 2}
NAMES = tuple(SIZES)
STATS = 128


def permute(x, names, move):
    dims = [SIZES[n] for n in names]
    pairs = []
    for place in np.ndindex(*dims):
        target = move(dict(zip(names, place)))
        pairs.append(
            (
                int(np.ravel_multi_index(place, dims)),
                int(np.ravel_multi_index([target[n] for n in names], dims)),
            )
        )
    return lax.ppermute(x, names, pairs)


def along_z(x, step):
    def move(at):
        place = (at["h"] * 8 + at["z"] + (step if at["c"] == 0 else -step)) % 16
        return {"z": place % 8, "c": at["c"], "h": place // 8}

    return permute(x, ("z", "c", "h"), move)


def other_core(x):
    return permute(x, ("c",), lambda at: {"c": 1 - at["c"]})


def swap_y(x):
    return lax.all_to_all(x, "y", split_axis=0, concat_axis=0, tiled=True)


def pack_kernel(order, content, rotary, out, *, block):
    heads, nope = content.shape[1:]
    left = heads * nope
    width = left + rotary.shape[1]
    row = lax.broadcasted_iota(jnp.int32, (out.shape[1], STATS), 0)
    number = jnp.where(row < block, order[0], order[1]).astype(jnp.float32).astype(out.dtype)
    for i in range(out.shape[0]):
        for h in range(heads):
            out[i, :, h * nope : (h + 1) * nope] = content[:, h, :]
        out[i, :, left:width] = rotary[...]
        out[i, :, width:] = number


def pack(order, content, rotary, block, copies):
    rows, heads, nope = content.shape
    width = heads * nope + rotary.shape[1] + STATS
    vmem = pl.BlockSpec(memory_space=pltpu.VMEM)
    return pl.pallas_call(
        functools.partial(pack_kernel, block=block),
        in_specs=[pl.BlockSpec(memory_space=pltpu.SMEM), vmem, vmem],
        out_specs=vmem,
        out_shape=jax.ShapeDtypeStruct((copies, rows, width), jnp.bfloat16),
    )(order, content, rotary)


def query_kernel(content, rotary, key_up, out):
    head = pl.program_id(0)
    latent = lax.dot_general(
        content[...], key_up[...], (((1,), (1,)), ((), ())), preferred_element_type=jnp.float32
    )
    out[0, :, : latent.shape[1]] = latent.astype(out.dtype)
    pair = rotary[...]
    half = pair.shape[1] // 2
    out[0, :, latent.shape[1] :] = jnp.where(head % 2 == 0, pair[:, :half], pair[:, half:])


def latent_queries(payload, key_up, heads, nope, rope):
    rows = payload.shape[0]
    latent = key_up.shape[0]
    return pl.pallas_call(
        query_kernel,
        grid=(heads,),
        in_specs=[
            pl.BlockSpec((rows, nope), lambda i: (0, i)),
            pl.BlockSpec((rows, 2 * rope), lambda i: (0, heads * nope // (2 * rope) + i // 2)),
            pl.BlockSpec((latent, nope), lambda i: (0, i)),
        ],
        out_specs=pl.BlockSpec((1, rows, latent + rope), lambda i: (i, 0, 0)),
        out_shape=jax.ShapeDtypeStruct((heads, rows, latent + rope), jnp.bfloat16),
        cost_estimate=pl.CostEstimate(
            flops=2 * heads * rows * latent * nope, bytes_accessed=8 * 1024 * 1024, transcendentals=0
        ),
    )(payload, payload, key_up)


def three_parts(x):
    parts = []
    for _ in range(3):
        part = x.astype(jnp.bfloat16).astype(jnp.float32)
        parts.append(part)
        x = x - part
    return parts


def read_stats(rows, heads):
    stats = rows[:, rows.shape[1] - STATS :].astype(jnp.float32)
    return stats[:, :heads] + stats[:, heads : 2 * heads] + stats[:, 2 * heads : 3 * heads]


def write_stats(rows, lse):
    heads = lse.shape[1]
    empty = jnp.zeros((lse.shape[0], STATS - 3 * heads), jnp.float32)
    rows[:, rows.shape[1] - STATS :] = jnp.concatenate(three_parts(lse) + [empty], axis=1).astype(
        rows.dtype
    )


def attend_kernel(
    starts, bases, limit_ref, query, *rest, shards, coef, latent, block, heads, groups, with_before
):
    *keys, value_up, before, out, mixed = rest
    group = pl.program_id(0)
    rows = heads * block
    width = keys[0].shape[2]
    limit = limit_ref[0]
    lowest, highest = bases[0], bases[0]
    for i in range(1, shards):
        lowest = jnp.minimum(lowest, bases[i])
        highest = jnp.maximum(highest, bases[i])

    def write(half, normal, lse):
        at = pl.ds(group * 2 * block + half * block, block)
        mixed[:, at, :] = normal.astype(mixed.dtype).reshape(heads, block, latent)
        lane = lax.broadcasted_iota(jnp.int32, (block, STATS), 1)
        parts = three_parts(lse)
        stats = jnp.zeros((block, STATS), jnp.float32)
        for k, part in enumerate(parts):
            for h in range(heads):
                stats = jnp.where(
                    lane == k * heads + h, part[h * block : (h + 1) * block, :], stats
                )
        out[at, out.shape[1] - STATS :] = stats.astype(out.dtype)

    def run(half, masked):
        rows_q = query[:, half * block : (half + 1) * block, :].reshape(rows, -1)
        k = jnp.concatenate([r[i] for r in keys for i in range(r.shape[0])], axis=1)
        s = jnp.dot(rows_q, k, preferred_element_type=jnp.float32)
        if masked:
            token = lax.broadcasted_iota(jnp.int32, (rows, width), 0) % block
            last = jnp.minimum(starts[group * 2 + half] + token, limit - 1)
            lane = lax.broadcasted_iota(jnp.int32, (rows, width), 1)
            s = jnp.concatenate(
                [
                    jnp.where(lane + bases[i] <= last, s[:, i * width : (i + 1) * width], NEG)
                    for i in range(shards)
                ],
                axis=1,
            )
        top = jnp.max(s, axis=1, keepdims=True)
        if masked:
            top = jnp.maximum(top, NEG / 10)
        weights = jnp.exp2(s * coef - top * coef)
        total = jnp.sum(weights, axis=1, keepdims=True)
        values = lax.dot_general(
            weights.astype(jnp.bfloat16),
            k[:latent],
            (((1,), (1,)), ((), ())),
            preferred_element_type=jnp.float32,
        )
        if masked:
            some = total > 0
            safe = jnp.where(some, total, 1.0)
            write(half, values / safe, jnp.where(some, top * coef + jnp.log2(safe), NEG))
        else:
            write(half, values / total, top * coef + jnp.log2(total))

    for half in range(2):
        start = starts[group * 2 + half]
        sure = highest + width - 1 <= jnp.minimum(start, limit - 1)
        some = lowest <= jnp.minimum(start + block - 1, limit - 1)

        @pl.when(sure)
        def _():
            run(half, False)

        @pl.when(jnp.logical_and(some, jnp.logical_not(sure)))
        def _():
            run(half, True)

        @pl.when(jnp.logical_not(some))
        def _():
            write(half, jnp.zeros((rows, latent), jnp.float32), jnp.full((rows, 1), NEG))

    @pl.when(group == groups - 1)
    def _():
        if with_before:
            old, new = read_stats(before, heads), read_stats(out, heads)
            top = jnp.maximum(old, new)
            old, new = jnp.exp2(old - top), jnp.exp2(new - top)
            total = old + new
            old, new = old / total, new / total
            write_stats(out, top + jnp.log2(total))
        for h in range(heads):
            cols = slice(h * 128, (h + 1) * 128)
            value = jnp.dot(mixed[h], value_up[:, cols], preferred_element_type=jnp.float32)
            if with_before:
                value = value * new[:, h : h + 1]
                value = value + before[:, cols].astype(jnp.float32) * old[:, h : h + 1]
            out[:, cols] = value.astype(out.dtype)


def attend(starts, bases, limit, query, keys, value_up, scale, before=None):
    heads, tokens, depth = query.shape
    latent, value_width = value_up.shape
    shards = sum(k.shape[0] for k in keys)
    groups = starts.shape[0] // 2
    per_group = tokens // groups
    whole = lambda shape: pl.BlockSpec(shape, lambda i, *_: (0,) * len(shape))
    kernel = functools.partial(
        attend_kernel,
        shards=shards,
        coef=scale * LOG2E,
        latent=latent,
        block=per_group // 2,
        heads=heads,
        groups=groups,
        with_before=before is not None,
    )
    if before is None:
        before = jnp.zeros((16, STATS), jnp.bfloat16)
    return pl.pallas_call(
        kernel,
        grid_spec=pltpu.PrefetchScalarGridSpec(
            num_scalar_prefetch=3,
            grid=(groups,),
            in_specs=[pl.BlockSpec((heads, per_group, depth), lambda i, *_: (0, i, 0))]
            + [whole(k.shape) for k in keys]
            + [whole(value_up.shape), whole(before.shape)],
            out_specs=whole((tokens, value_width + STATS)),
            scratch_shapes=[pltpu.VMEM((heads, tokens, latent), jnp.bfloat16)],
        ),
        out_shape=jax.ShapeDtypeStruct((tokens, value_width + STATS), jnp.bfloat16),
        compiler_params=pltpu.CompilerParams(vmem_limit_bytes=48 * 1024 * 1024),
    )(starts, bases, limit, query, *keys, value_up, before)


def merge_kernel(parts, out, *, heads, sources):
    width = out.shape[2]
    each = width // heads
    lses = [read_stats(parts.at[s], heads) for s in range(sources)]
    top = functools.reduce(jnp.maximum, lses)
    weights = [jnp.exp2(v - top) for v in lses]
    total = functools.reduce(jnp.add, weights)
    weights = [w / total for w in weights]
    for h in range(heads):
        cols = slice(h * each, (h + 1) * each)
        value = functools.reduce(
            jnp.add,
            [
                weights[s][:, h : h + 1] * parts[s, :, cols].astype(jnp.float32)
                for s in range(sources)
            ],
        ).astype(out.dtype)
        for i in range(out.shape[0]):
            out[i, :, cols] = value


def merge(parts, heads, copies):
    sources, tokens, width = parts.shape
    return pl.pallas_call(
        functools.partial(merge_kernel, heads=heads, sources=sources),
        out_shape=jax.ShapeDtypeStruct((copies, tokens, width - STATS), jnp.bfloat16),
    )(parts)


def per_device(
    query_content,
    query_rotary,
    key_cache,
    key_up,
    value_up,
    output_weight,
    query_start,
    key_limit,
    block_order,
):
    tokens, heads, nope = query_content.shape
    latent = key_up.shape[0]
    rope = query_rotary.shape[1] // heads
    value_dim = value_up.shape[2]
    columns = output_weight.shape[1]
    block = tokens // 2
    scale = 1.0 / math.sqrt(nope + rope)
    shard = key_cache.shape[1]
    y, z, c, h = (lax.axis_index(n) for n in ("y", "z", "c", "h"))

    weight = lax.all_gather(output_weight.T, "z", axis=0, tiled=True)

    packed = pack(block_order, query_content, query_rotary, block, 4)

    pair = jnp.stack([key_cache, other_core(key_cache)])
    one, two = along_z(pair, 1), along_z(pair, 2)
    two, _ = lax.optimization_barrier((two, packed))
    near = jnp.concatenate([one, two], axis=0)
    near_swapped = other_core(near)
    three, four = along_z(two, 1), along_z(two[:1], 2)

    payload = swap_y(packed).reshape(4 * tokens, -1)
    starts = query_start[0] + payload[::block, -1].astype(jnp.int32) * block
    queries = latent_queries(payload, key_up.reshape(latent, heads * nope), heads, nope, rope)

    side = 1 - 2 * c

    def bases_of(steps, cores):
        steps, cores = np.array(steps, np.int32), np.array(cores, np.int32)
        place = (y * 8 + (z - side * steps) % 8) * 2 + (c + cores) % 2
        return place.astype(jnp.int32) * shard

    attend_part = functools.partial(
        attend, starts, limit=key_limit, query=queries, scale=scale,
        value_up=value_up.reshape(latent, heads * value_dim),
    )
    partial = attend_part(
        bases_of([0, 0, 1, 1, 2, 2, -1, -1, -2, -2], [0, 1, 0, 1, 0, 1, 1, 0, 1, 0]),
        keys=[pair, near, near_swapped],
    )
    three, four, partial = lax.optimization_barrier((three, four, partial))
    far = jnp.concatenate([three, four], axis=0)
    partial = attend_part(
        bases_of([3, 3, 4, -3, -3, -4], [0, 1, 0, 1, 0, 1]),
        keys=[far, other_core(far)],
        before=partial,
    )
    values = merge(swap_y(partial.reshape(4, tokens, -1)), heads, 4)
    values, weight = lax.optimization_barrier((values, weight))
    weights = [weight, other_core(weight)]

    rows = swap_y(values).reshape(4 * tokens, -1)
    product = jnp.concatenate(
        [
            lax.dot_general(
                rows, w, (((1,), (1,)), ((), ())), preferred_element_type=jnp.float32
            ).astype(jnp.bfloat16)
            for w in weights
        ],
        axis=1,
    )
    share = tokens // 8
    width = 16 * columns
    product = lax.all_to_all(
        product.reshape(16, 2 * share, width), ("y", "x"), split_axis=0, concat_axis=0, tiled=True
    )
    summed = jnp.sum(product.reshape(4, 4, 2, share, width).astype(jnp.float32), axis=1)
    mine = jnp.where(h == 0, summed[:, 0], summed[:, 1])
    theirs = jnp.where(h == 0, summed[:, 1], summed[:, 0]).astype(jnp.bfloat16)
    got = permute(theirs, ("h",), lambda at: {"h": 1 - at["h"]})
    total = (mine + got.astype(jnp.float32)).astype(jnp.bfloat16)
    total = total.reshape(4, share, 2, 8, columns)
    total = jnp.where(c == 0, total, total[:, :, ::-1])
    return total.transpose(1, 0, 3, 2, 4).reshape(share, 4 * width)


def solution(mesh):
    fine = Mesh(mesh.devices.reshape(tuple(SIZES.values())), NAMES)
    seq, head = ("y", "z", "c"), ("x", "h")
    in_specs = (
        P(seq, head, None),
        P(seq, head),
        P(None, seq),
        P(None, head, None),
        P(None, head, None),
        P(head, seq),
        P(),
        P(),
        P(seq),
    )
    return jax.shard_map(
        per_device, mesh=fine, in_specs=in_specs, out_specs=P(seq + head, None), check_vma=False
    )
```

```python
import functools
import math

import jax
import jax.numpy as jnp
import numpy as np
from jax import lax
from jax.experimental import pallas as pl
from jax.experimental.pallas import tpu as pltpu
from jax.sharding import Mesh, PartitionSpec as P

NEG = -1e30
LOG2E = 1.4426950408889634
SIZES = {"y": 4, "z": 8, "c": 2, "x": 4, "h": 2}
NAMES = tuple(SIZES)
STATS = 128


def permute(x, names, move):
    dims = [SIZES[n] for n in names]
    pairs = []
    for place in np.ndindex(*dims):
        target = move(dict(zip(names, place)))
        pairs.append(
            (
                int(np.ravel_multi_index(place, dims)),
                int(np.ravel_multi_index([target[n] for n in names], dims)),
            )
        )
    return lax.ppermute(x, names, pairs)


def along_z(x, step):
    def move(at):
        place = (at["h"] * 8 + at["z"] + (step if at["c"] == 0 else -step)) % 16
        return {"z": place % 8, "c": at["c"], "h": place // 8}

    return permute(x, ("z", "c", "h"), move)


def other_core(x):
    return permute(x, ("c",), lambda at: {"c": 1 - at["c"]})


def swap_y(x):
    return lax.all_to_all(x, "y", split_axis=0, concat_axis=0, tiled=True)


def pack_kernel(order, content, rotary, out, *, block):
    heads, nope = content.shape[1:]
    left = heads * nope
    width = left + rotary.shape[1]
    row = lax.broadcasted_iota(jnp.int32, (out.shape[1], STATS), 0)
    number = jnp.where(row < block, order[0], order[1]).astype(jnp.float32).astype(out.dtype)
    for i in range(out.shape[0]):
        for h in range(heads):
            out[i, :, h * nope : (h + 1) * nope] = content[:, h, :]
        out[i, :, left:width] = rotary[...]
        out[i, :, width:] = number


def pack(order, content, rotary, block, copies):
    rows, heads, nope = content.shape
    width = heads * nope + rotary.shape[1] + STATS
    vmem = pl.BlockSpec(memory_space=pltpu.VMEM)
    return pl.pallas_call(
        functools.partial(pack_kernel, block=block),
        in_specs=[pl.BlockSpec(memory_space=pltpu.SMEM), vmem, vmem],
        out_specs=vmem,
        out_shape=jax.ShapeDtypeStruct((copies, rows, width), jnp.bfloat16),
    )(order, content, rotary)


def query_kernel(payload, key_up, out, *, heads, nope, rope):
    latent = key_up.shape[0]
    for h in range(heads):
        cols = slice(h * nope, (h + 1) * nope)
        out[h, :latent, :] = lax.dot_general(
            key_up[:, cols],
            payload[:, cols],
            (((1,), (1,)), ((), ())),
            preferred_element_type=jnp.float32,
        ).astype(out.dtype)
    for p in range(heads // 2):
        cols = slice(heads * nope + 2 * p * rope, heads * nope + 2 * (p + 1) * rope)
        both = payload[:, cols].astype(jnp.float32).T.astype(out.dtype)
        out[2 * p, latent:, :] = both[:rope]
        out[2 * p + 1, latent:, :] = both[rope:]


def latent_queries(payload, key_up, heads, nope, rope):
    rows = payload.shape[0]
    latent = key_up.shape[0]
    return pl.pallas_call(
        functools.partial(query_kernel, heads=heads, nope=nope, rope=rope),
        out_shape=jax.ShapeDtypeStruct((heads, latent + rope, rows), jnp.bfloat16),
        compiler_params=pltpu.CompilerParams(vmem_limit_bytes=48 * 1024 * 1024),
        cost_estimate=pl.CostEstimate(
            flops=2 * heads * rows * latent * nope, bytes_accessed=8 * 1024 * 1024, transcendentals=0
        ),
    )(payload, key_up)


def three_parts(x):
    parts = []
    for _ in range(3):
        part = x.astype(jnp.bfloat16).astype(jnp.float32)
        parts.append(part)
        x = x - part
    return parts


def read_stats(rows, heads):
    stats = rows[:, rows.shape[1] - STATS :].astype(jnp.float32)
    return stats[:, :heads] + stats[:, heads : 2 * heads] + stats[:, 2 * heads : 3 * heads]


def attend_kernel(
    starts, bases, limit_ref, query, *rest, shards, coef, block, some, with_before
):
    *keys, value_up, before, out, turned, lses, olds = rest
    first = pl.program_id(0) * some
    heads, tokens = lses.shape
    value_dim, latent = value_up.shape[1:]
    width = keys[0].shape[2]
    tiles = [(r, i) for r in keys for i in range(r.shape[0])]
    columns = some * tokens
    limit = limit_ref[0]
    left = out.shape[1] - STATS

    @pl.when(first == 0)
    def _():
        for n, (r, i) in enumerate(tiles):
            turned[n * width : (n + 1) * width, :] = r[i].T
        if with_before:
            stats = before[:, left:].astype(jnp.float32).T
            olds[...] = stats[:heads] + stats[heads : 2 * heads] + stats[2 * heads : 3 * heads]

    highest, nearest = bases[0], starts[0]
    for i in range(1, shards):
        highest = jnp.maximum(highest, bases[i])
    for i in range(1, tokens // block):
        nearest = jnp.minimum(nearest, starts[i])
    sure = highest + width - 1 <= jnp.minimum(nearest, limit - 1)

    def run(masked):
        q = jnp.concatenate([query[i] for i in range(some)], axis=1)
        s = jnp.dot(turned[...], q, preferred_element_type=jnp.float32)
        if masked:
            token = lax.broadcasted_iota(jnp.int32, (1, columns), 1) % tokens
            last = token % block
            for i in range(tokens // block):
                last = last + jnp.where(token // block == i, starts[i], 0)
            last = jnp.minimum(last, limit - 1)
            row = lax.broadcasted_iota(jnp.int32, (width, columns), 0)
            s = jnp.concatenate(
                [
                    jnp.where(row + bases[n] <= last, s[n * width : (n + 1) * width], NEG)
                    for n in range(shards)
                ],
                axis=0,
            )
        top = jnp.max(s, axis=0, keepdims=True)
        if masked:
            top = jnp.maximum(top, NEG / 10)
        weights = jnp.exp2(s * coef - top * coef)
        total = jnp.sum(weights, axis=0, keepdims=True)
        k = jnp.concatenate([r[i, :latent] for r, i in tiles], axis=1)
        values = jnp.dot(k, weights.astype(jnp.bfloat16), preferred_element_type=jnp.float32)
        if masked:
            seen = total > 0
            total = jnp.where(seen, total, 1.0)
            lse = jnp.where(seen, top * coef + jnp.log2(total), NEG)
        else:
            lse = top * coef + jnp.log2(total)
        mixed = (values * (1.0 / total)).astype(jnp.bfloat16)
        mine = [lse[:, i * tokens : (i + 1) * tokens] for i in range(some)]
        new = [None] * some
        if with_before:
            old = []
            for i in range(some):
                past = olds[pl.ds(first + i, 1), :]
                peak = jnp.maximum(past, mine[i])
                a, b = jnp.exp2(past - peak), jnp.exp2(mine[i] - peak)
                old.append(a / (a + b))
                new[i] = b / (a + b)
                mine[i] = peak + jnp.log2(a + b)
            old = jnp.concatenate(old + [jnp.zeros((8 - some, tokens), jnp.float32)], axis=0).T
        for i in range(some):
            lses[pl.ds(first + i, 1), :] = mine[i]
            value = jnp.dot(
                value_up[i], mixed[:, i * tokens : (i + 1) * tokens], preferred_element_type=jnp.float32
            )
            if with_before:
                value = value * new[i]
            value = value.T
            cols = pl.ds(pl.multiple_of((first + i) * value_dim, value_dim), value_dim)
            if with_before:
                value = value + before[:, cols].astype(jnp.float32) * old[:, i : i + 1]
            out[:, cols] = value.astype(out.dtype)

    @pl.when(sure)
    def _():
        run(False)

    @pl.when(jnp.logical_not(sure))
    def _():
        run(True)

    @pl.when(first + some == heads)
    def _():
        empty = jnp.zeros((STATS - 3 * heads, tokens), jnp.float32)
        stats = jnp.concatenate(three_parts(lses[...]) + [empty], axis=0)
        out[:, left:] = stats.T.astype(out.dtype)


def attend(starts, bases, limit, query, keys, value_up, scale, before=None, some=4):
    heads, depth, tokens = query.shape
    value_dim, latent = value_up.shape[1:]
    shards = sum(k.shape[0] for k in keys)
    width = keys[0].shape[2]
    whole = lambda shape: pl.BlockSpec(shape, lambda i, *_: (0,) * len(shape))
    kernel = functools.partial(
        attend_kernel,
        shards=shards,
        coef=scale * LOG2E,
        block=tokens // starts.shape[0],
        some=some,
        with_before=before is not None,
    )
    if before is None:
        before = jnp.zeros((16, STATS), jnp.bfloat16)
    return pl.pallas_call(
        kernel,
        grid_spec=pltpu.PrefetchScalarGridSpec(
            num_scalar_prefetch=3,
            grid=(heads // some,),
            in_specs=[pl.BlockSpec((some, depth, tokens), lambda i, *_: (i, 0, 0))]
            + [whole(k.shape) for k in keys]
            + [pl.BlockSpec((some, value_dim, latent), lambda i, *_: (i, 0, 0))]
            + [whole(before.shape)],
            out_specs=whole((tokens, heads * value_dim + STATS)),
            scratch_shapes=[
                pltpu.VMEM((shards * width, depth), jnp.bfloat16),
                pltpu.VMEM((heads, tokens), jnp.float32),
                pltpu.VMEM((heads, tokens), jnp.float32),
            ],
        ),
        out_shape=jax.ShapeDtypeStruct((tokens, heads * value_dim + STATS), jnp.bfloat16),
        compiler_params=pltpu.CompilerParams(vmem_limit_bytes=48 * 1024 * 1024),
    )(starts, bases, limit, query, *keys, value_up, before)


def merge_kernel(parts, out, *, heads, sources):
    width = out.shape[2]
    each = width // heads
    lses = [read_stats(parts.at[s], heads) for s in range(sources)]
    top = functools.reduce(jnp.maximum, lses)
    weights = [jnp.exp2(v - top) for v in lses]
    total = functools.reduce(jnp.add, weights)
    weights = [w / total for w in weights]
    for h in range(heads):
        cols = slice(h * each, (h + 1) * each)
        value = functools.reduce(
            jnp.add,
            [
                weights[s][:, h : h + 1] * parts[s, :, cols].astype(jnp.float32)
                for s in range(sources)
            ],
        ).astype(out.dtype)
        for i in range(out.shape[0]):
            out[i, :, cols] = value


def merge(parts, heads, copies):
    sources, tokens, width = parts.shape
    return pl.pallas_call(
        functools.partial(merge_kernel, heads=heads, sources=sources),
        out_shape=jax.ShapeDtypeStruct((copies, tokens, width - STATS), jnp.bfloat16),
    )(parts)


def per_device(
    query_content,
    query_rotary,
    key_cache,
    key_up,
    value_up,
    output_weight,
    query_start,
    key_limit,
    block_order,
):
    tokens, heads, nope = query_content.shape
    latent = key_up.shape[0]
    rope = query_rotary.shape[1] // heads
    columns = output_weight.shape[1]
    block = tokens // 2
    scale = 1.0 / math.sqrt(nope + rope)
    shard = key_cache.shape[1]
    y, z, c, h = (lax.axis_index(n) for n in ("y", "z", "c", "h"))

    weight = lax.all_gather(output_weight.T, "z", axis=0, tiled=True)

    packed = pack(block_order, query_content, query_rotary, block, 4)

    pair = jnp.stack([key_cache, other_core(key_cache)])
    one, two = along_z(pair, 1), along_z(pair, 2)
    key_up = key_up.reshape(latent, heads * nope)
    value_up = value_up.transpose(1, 2, 0)
    two, _, key_up, value_up = lax.optimization_barrier((two, packed, key_up, value_up))
    near = jnp.concatenate([one, two], axis=0)
    near_swapped = other_core(near)
    three, four = along_z(two, 1), along_z(two[:1], 2)

    payload = swap_y(packed).reshape(4 * tokens, -1)
    starts = query_start[0] + payload[::block, -1].astype(jnp.int32) * block
    queries = latent_queries(payload, key_up, heads, nope, rope)

    side = 1 - 2 * c

    def bases_of(steps, cores):
        steps, cores = np.array(steps, np.int32), np.array(cores, np.int32)
        place = (y * 8 + (z - side * steps) % 8) * 2 + (c + cores) % 2
        return place.astype(jnp.int32) * shard

    attend_part = functools.partial(
        attend, starts, limit=key_limit, query=queries, scale=scale,
        value_up=value_up,
    )
    partial = attend_part(
        bases_of([0, 0, 1, 1, 2, 2, -1, -1, -2, -2], [0, 1, 0, 1, 0, 1, 1, 0, 1, 0]),
        keys=[pair, near, near_swapped],
    )
    three, four, partial = lax.optimization_barrier((three, four, partial))
    far = jnp.concatenate([three, four], axis=0)
    partial = attend_part(
        bases_of([3, 3, 4, -3, -3, -4], [0, 1, 0, 1, 0, 1]),
        keys=[far, other_core(far)],
        before=partial,
    )
    values = merge(swap_y(partial.reshape(4, tokens, -1)), heads, 4)
    values, weight = lax.optimization_barrier((values, weight))
    weights = [weight, other_core(weight)]

    rows = swap_y(values).reshape(4 * tokens, -1)
    product = jnp.concatenate(
        [
            lax.dot_general(
                rows, w, (((1,), (1,)), ((), ())), preferred_element_type=jnp.float32
            ).astype(jnp.bfloat16)
            for w in weights
        ],
        axis=1,
    )
    share = tokens // 8
    width = 16 * columns
    product = lax.all_to_all(
        product.reshape(16, 2 * share, width), ("y", "x"), split_axis=0, concat_axis=0, tiled=True
    )
    summed = jnp.sum(product.reshape(4, 4, 2, share, width).astype(jnp.float32), axis=1)
    mine = jnp.where(h == 0, summed[:, 0], summed[:, 1])
    theirs = jnp.where(h == 0, summed[:, 1], summed[:, 0]).astype(jnp.bfloat16)
    got = permute(theirs, ("h",), lambda at: {"h": 1 - at["h"]})
    total = (mine + got.astype(jnp.float32)).astype(jnp.bfloat16)
    total = total.reshape(4, share, 2, 8, columns)
    total = jnp.where(c == 0, total, total[:, :, ::-1])
    return total.transpose(1, 0, 3, 2, 4).reshape(share, 4 * width)


def solution(mesh):
    fine = Mesh(mesh.devices.reshape(tuple(SIZES.values())), NAMES)
    seq, head = ("y", "z", "c"), ("x", "h")
    in_specs = (
        P(seq, head, None),
        P(seq, head),
        P(None, seq),
        P(None, head, None),
        P(None, head, None),
        P(head, seq),
        P(),
        P(),
        P(seq),
    )
    return jax.shard_map(
        per_device, mesh=fine, in_specs=in_specs, out_specs=P(seq + head, None), check_vma=False
    )
```

```python
import functools
import math

import jax
import jax.numpy as jnp
import numpy as np
from jax import lax
from jax.experimental import pallas as pl
from jax.experimental.pallas import tpu as pltpu
from jax.sharding import Mesh, PartitionSpec as P

NEG = -1e30
LOG2E = 1.4426950408889634
SIZES = {"y": 4, "z": 8, "c": 2, "x": 4, "h": 2}
NAMES = tuple(SIZES)
STATS = 128


def permute(x, names, move):
    dims = [SIZES[n] for n in names]
    pairs = []
    for place in np.ndindex(*dims):
        target = move(dict(zip(names, place)))
        pairs.append(
            (
                int(np.ravel_multi_index(place, dims)),
                int(np.ravel_multi_index([target[n] for n in names], dims)),
            )
        )
    return lax.ppermute(x, names, pairs)


def along_z(x, step):
    def move(at):
        place = (at["h"] * 8 + at["z"] + (step if at["c"] == 0 else -step)) % 16
        return {"z": place % 8, "c": at["c"], "h": place // 8}

    return permute(x, ("z", "c", "h"), move)


def other_core(x):
    return permute(x, ("c",), lambda at: {"c": 1 - at["c"]})


def swap_y(x):
    return lax.all_to_all(x, "y", split_axis=0, concat_axis=0, tiled=True)


def pack_kernel(order, content, rotary, out, *, block):
    heads, nope = content.shape[1:]
    left = heads * nope
    width = left + rotary.shape[1]
    row = lax.broadcasted_iota(jnp.int32, (out.shape[1], STATS), 0)
    number = jnp.where(row < block, order[0], order[1]).astype(jnp.float32).astype(out.dtype)
    for i in range(out.shape[0]):
        for h in range(heads):
            out[i, :, h * nope : (h + 1) * nope] = content[:, h, :]
        out[i, :, left:width] = rotary[...]
        out[i, :, width:] = number


def pack(order, content, rotary, block, copies):
    rows, heads, nope = content.shape
    width = heads * nope + rotary.shape[1] + STATS
    vmem = pl.BlockSpec(memory_space=pltpu.VMEM)
    return pl.pallas_call(
        functools.partial(pack_kernel, block=block),
        in_specs=[pl.BlockSpec(memory_space=pltpu.SMEM), vmem, vmem],
        out_specs=vmem,
        out_shape=jax.ShapeDtypeStruct((copies, rows, width), jnp.bfloat16),
    )(order, content, rotary)


def query_kernel(start, payload, key_up, out, starts, *, heads, nope, rope):
    latent = key_up.shape[0]
    block = payload.shape[0] // starts.shape[0]
    for i in range(starts.shape[0]):
        number = payload[i * block : (i + 1) * block, payload.shape[1] - STATS :]
        starts[i] = start[0] + jnp.max(number.astype(jnp.float32)).astype(jnp.int32) * block
    for h in range(heads):
        cols = slice(h * nope, (h + 1) * nope)
        out[h, :latent, :] = lax.dot_general(
            key_up[:, cols],
            payload[:, cols],
            (((1,), (1,)), ((), ())),
            preferred_element_type=jnp.float32,
        ).astype(out.dtype)
    for p in range(heads // 2):
        cols = slice(heads * nope + 2 * p * rope, heads * nope + 2 * (p + 1) * rope)
        both = payload[:, cols].astype(jnp.float32).T.astype(out.dtype)
        out[2 * p, latent:, :] = both[:rope]
        out[2 * p + 1, latent:, :] = both[rope:]


def latent_queries(start, payload, key_up, heads, nope, rope, blocks):
    rows = payload.shape[0]
    latent = key_up.shape[0]
    smem, vmem = pl.BlockSpec(memory_space=pltpu.SMEM), pl.BlockSpec(memory_space=pltpu.VMEM)
    return pl.pallas_call(
        functools.partial(query_kernel, heads=heads, nope=nope, rope=rope),
        in_specs=[smem, vmem, vmem],
        out_specs=[vmem, smem],
        out_shape=[
            jax.ShapeDtypeStruct((heads, latent + rope, rows), jnp.bfloat16),
            jax.ShapeDtypeStruct((blocks,), jnp.int32),
        ],
        compiler_params=pltpu.CompilerParams(vmem_limit_bytes=48 * 1024 * 1024),
        cost_estimate=pl.CostEstimate(
            flops=2 * heads * rows * latent * nope, bytes_accessed=8 * 1024 * 1024, transcendentals=0
        ),
    )(start, payload, key_up)


def three_parts(x):
    parts = []
    for _ in range(3):
        part = x.astype(jnp.bfloat16).astype(jnp.float32)
        parts.append(part)
        x = x - part
    return parts


def read_stats(rows, heads):
    stats = rows[:, rows.shape[1] - STATS :].astype(jnp.float32)
    return stats[:, :heads] + stats[:, heads : 2 * heads] + stats[:, 2 * heads : 3 * heads]


def attend_kernel(
    starts, place, query, *rest, shards, coef, block, some, with_before
):
    *keys, value_up, before, out, turned, lses, olds = rest
    first = pl.program_id(0) * some
    heads, tokens = lses.shape
    value_dim, latent = value_up.shape[1:]
    width = keys[0].shape[2]
    tiles = [(r, i) for r in keys for i in range(r.shape[0])]
    columns = some * tokens
    limit = place[3]
    side = 1 - 2 * place[2]
    bases = [
        ((place[0] * 8 + (place[1] + 8 - side * step) % 8) * 2 + core) * width for step, core in shards
    ]
    left = out.shape[1] - STATS

    @pl.when(first == 0)
    def _():
        for n, (r, i) in enumerate(tiles):
            turned[n * width : (n + 1) * width, :] = r[i].T
        if with_before:
            stats = before[:, left:].astype(jnp.float32).T
            olds[...] = stats[:heads] + stats[heads : 2 * heads] + stats[2 * heads : 3 * heads]

    highest, nearest = bases[0], starts[0]
    for i in range(1, len(shards)):
        highest = jnp.maximum(highest, bases[i])
    for i in range(1, tokens // block):
        nearest = jnp.minimum(nearest, starts[i])
    sure = highest + width - 1 <= jnp.minimum(nearest, limit - 1)

    def run(masked):
        q = jnp.concatenate([query[i] for i in range(some)], axis=1)
        s = jnp.dot(turned[...], q, preferred_element_type=jnp.float32)
        if masked:
            token = lax.broadcasted_iota(jnp.int32, (1, columns), 1) % tokens
            last = token % block
            for i in range(tokens // block):
                last = last + jnp.where(token // block == i, starts[i], 0)
            last = jnp.minimum(last, limit - 1)
            row = lax.broadcasted_iota(jnp.int32, (width, columns), 0)
            s = jnp.concatenate(
                [
                    jnp.where(row + bases[n] <= last, s[n * width : (n + 1) * width], NEG)
                    for n in range(len(shards))
                ],
                axis=0,
            )
        top = jnp.max(s, axis=0, keepdims=True)
        if masked:
            top = jnp.maximum(top, NEG / 10)
        weights = jnp.exp2(s * coef - top * coef)
        total = jnp.sum(weights, axis=0, keepdims=True)
        k = jnp.concatenate([r[i, :latent] for r, i in tiles], axis=1)
        values = jnp.dot(k, weights.astype(jnp.bfloat16), preferred_element_type=jnp.float32)
        if masked:
            seen = total > 0
            total = jnp.where(seen, total, 1.0)
            lse = jnp.where(seen, top * coef + jnp.log2(total), NEG)
        else:
            lse = top * coef + jnp.log2(total)
        mixed = (values * (1.0 / total)).astype(jnp.bfloat16)
        mine = [lse[:, i * tokens : (i + 1) * tokens] for i in range(some)]
        new = [None] * some
        if with_before:
            old = []
            for i in range(some):
                past = olds[pl.ds(first + i, 1), :]
                peak = jnp.maximum(past, mine[i])
                a, b = jnp.exp2(past - peak), jnp.exp2(mine[i] - peak)
                old.append(a / (a + b))
                new[i] = b / (a + b)
                mine[i] = peak + jnp.log2(a + b)
            old = jnp.concatenate(old + [jnp.zeros((8 - some, tokens), jnp.float32)], axis=0).T
        for i in range(some):
            lses[pl.ds(first + i, 1), :] = mine[i]
            value = jnp.dot(
                value_up[i], mixed[:, i * tokens : (i + 1) * tokens], preferred_element_type=jnp.float32
            )
            if with_before:
                value = value * new[i]
            value = value.T
            cols = pl.ds(pl.multiple_of((first + i) * value_dim, value_dim), value_dim)
            if with_before:
                value = value + before[:, cols].astype(jnp.float32) * old[:, i : i + 1]
            out[:, cols] = value.astype(out.dtype)

    @pl.when(sure)
    def _():
        run(False)

    @pl.when(jnp.logical_not(sure))
    def _():
        run(True)

    @pl.when(first + some == heads)
    def _():
        empty = jnp.zeros((STATS - 3 * heads, tokens), jnp.float32)
        stats = jnp.concatenate(three_parts(lses[...]) + [empty], axis=0)
        out[:, left:] = stats.T.astype(out.dtype)


def attend(starts, place, query, keys, shards, value_up, scale, before=None, some=4):
    heads, depth, tokens = query.shape
    value_dim, latent = value_up.shape[1:]
    width = keys[0].shape[2]
    whole = lambda shape: pl.BlockSpec(shape, lambda i, *_: (0,) * len(shape))
    kernel = functools.partial(
        attend_kernel,
        shards=shards,
        coef=scale * LOG2E,
        block=tokens // starts.shape[0],
        some=some,
        with_before=before is not None,
    )
    if before is None:
        before = jnp.zeros((16, STATS), jnp.bfloat16)
    return pl.pallas_call(
        kernel,
        grid_spec=pltpu.PrefetchScalarGridSpec(
            num_scalar_prefetch=2,
            grid=(heads // some,),
            in_specs=[pl.BlockSpec((some, depth, tokens), lambda i, *_: (i, 0, 0))]
            + [whole(k.shape) for k in keys]
            + [pl.BlockSpec((some, value_dim, latent), lambda i, *_: (i, 0, 0))]
            + [whole(before.shape)],
            out_specs=whole((tokens, heads * value_dim + STATS)),
            scratch_shapes=[
                pltpu.VMEM((len(shards) * width, depth), jnp.bfloat16),
                pltpu.VMEM((heads, tokens), jnp.float32),
                pltpu.VMEM((heads, tokens), jnp.float32),
            ],
        ),
        out_shape=jax.ShapeDtypeStruct((tokens, heads * value_dim + STATS), jnp.bfloat16),
        compiler_params=pltpu.CompilerParams(vmem_limit_bytes=48 * 1024 * 1024),
    )(starts, place, query, *keys, value_up, before)


def merge_kernel(parts, out, *, heads, sources):
    width = out.shape[2]
    each = width // heads
    lses = [read_stats(parts.at[s], heads) for s in range(sources)]
    top = functools.reduce(jnp.maximum, lses)
    weights = [jnp.exp2(v - top) for v in lses]
    total = functools.reduce(jnp.add, weights)
    weights = [w / total for w in weights]
    for h in range(heads):
        cols = slice(h * each, (h + 1) * each)
        value = functools.reduce(
            jnp.add,
            [
                weights[s][:, h : h + 1] * parts[s, :, cols].astype(jnp.float32)
                for s in range(sources)
            ],
        ).astype(out.dtype)
        for i in range(out.shape[0]):
            out[i, :, cols] = value


def merge(parts, heads, copies):
    sources, tokens, width = parts.shape
    return pl.pallas_call(
        functools.partial(merge_kernel, heads=heads, sources=sources),
        out_shape=jax.ShapeDtypeStruct((copies, tokens, width - STATS), jnp.bfloat16),
    )(parts)


def product_kernel(rows, mine, other, out):
    step = pl.program_id(0)
    width = mine.shape[0]
    for n, weight in enumerate((mine, other)):
        cols = pl.ds(pl.multiple_of(step * width + n * out.shape[1] // 2, width), width)
        out[:, cols] = lax.dot_general(
            rows[...], weight[...], (((1,), (1,)), ((), ())), preferred_element_type=jnp.float32
        ).astype(out.dtype)


def project(rows, mine, other, width=128):
    tokens, depth = rows.shape
    columns = mine.shape[0]
    return pl.pallas_call(
        product_kernel,
        grid=(columns // width,),
        in_specs=[
            pl.BlockSpec((tokens, depth), lambda i: (0, 0)),
            pl.BlockSpec((width, depth), lambda i: (i, 0)),
            pl.BlockSpec((width, depth), lambda i: (i, 0)),
        ],
        out_specs=pl.BlockSpec((tokens, 2 * columns), lambda i: (0, 0)),
        out_shape=jax.ShapeDtypeStruct((tokens, 2 * columns), jnp.bfloat16),
    )(rows, mine, other)


def per_device(
    query_content,
    query_rotary,
    key_cache,
    key_up,
    value_up,
    output_weight,
    query_start,
    key_limit,
    block_order,
):
    tokens, heads, nope = query_content.shape
    latent = key_up.shape[0]
    rope = query_rotary.shape[1] // heads
    columns = output_weight.shape[1]
    block = tokens // 2
    scale = 1.0 / math.sqrt(nope + rope)
    y, z, c, h = (lax.axis_index(n) for n in ("y", "z", "c", "h"))

    weight = lax.all_gather(output_weight.T, "z", axis=0, tiled=True)

    packed = pack(block_order, query_content, query_rotary, block, 4)

    pair = lax.all_gather(key_cache, "c", axis=0, tiled=True).reshape(2, *key_cache.shape)
    one, two = along_z(pair, 1), along_z(pair, 2)
    key_up = key_up.reshape(latent, heads * nope)
    value_up = value_up.transpose(1, 2, 0)
    place = jnp.concatenate([jnp.stack([y, z, c]).astype(jnp.int32), key_limit])
    two, _, key_up, value_up, place = lax.optimization_barrier(
        (two, packed, key_up, value_up, place)
    )
    near = jnp.concatenate([one, two], axis=0)
    near_swapped = other_core(near)
    three, four = along_z(two, 1), along_z(two, 2)

    payload = swap_y(packed).reshape(4 * tokens, -1)
    queries, starts = latent_queries(query_start, payload, key_up, heads, nope, rope, 8)

    attend_part = functools.partial(
        attend, starts, place, queries, scale=scale, value_up=value_up
    )
    pairs = lambda steps: [(step, core) for step in steps for core in (0, 1)]
    partial = attend_part(keys=[pair, near, near_swapped], shards=pairs((0, 1, 2, -1, -2)))
    three, four, partial = lax.optimization_barrier((three, four, partial))
    partial = attend_part(
        keys=[four, three, other_core(three)], shards=pairs((4, 3, -3)), before=partial
    )
    values = merge(swap_y(partial.reshape(4, tokens, -1)), heads, 4)
    values, weight = lax.optimization_barrier((values, weight))
    weights = [weight, other_core(weight)]

    rows = swap_y(values).reshape(4 * tokens, -1)
    product = project(rows, *weights)
    share = tokens // 8
    width = 16 * columns
    product = lax.all_to_all(
        product.reshape(16, 2 * share, width), ("y", "x"), split_axis=0, concat_axis=0, tiled=True
    )
    summed = jnp.sum(product.reshape(4, 4, 2, share, width).astype(jnp.float32), axis=1)
    mine = jnp.where(h == 0, summed[:, 0], summed[:, 1])
    theirs = jnp.where(h == 0, summed[:, 1], summed[:, 0]).astype(jnp.bfloat16)
    got = permute(theirs, ("h",), lambda at: {"h": 1 - at["h"]})
    total = (mine + got.astype(jnp.float32)).astype(jnp.bfloat16)
    total = total.reshape(4, share, 2, 8, columns)
    total = jnp.where(c == 0, total, total[:, :, ::-1])
    return total.transpose(1, 0, 3, 2, 4).reshape(share, 4 * width)


def solution(mesh):
    fine = Mesh(mesh.devices.reshape(tuple(SIZES.values())), NAMES)
    seq, head = ("y", "z", "c"), ("x", "h")
    in_specs = (
        P(seq, head, None),
        P(seq, head),
        P(None, seq),
        P(None, head, None),
        P(None, head, None),
        P(head, seq),
        P(),
        P(),
        P(seq),
    )
    return jax.shard_map(
        per_device, mesh=fine, in_specs=in_specs, out_specs=P(seq + head, None), check_vma=False
    )
```

```python
import functools
import math

import jax
import jax.numpy as jnp
import numpy as np
from jax import lax
from jax.experimental import pallas as pl
from jax.experimental.pallas import tpu as pltpu
from jax.sharding import Mesh, PartitionSpec as P

NEG = -1e30
LOG2E = 1.4426950408889634
SIZES = {"y": 4, "z": 8, "c": 2, "x": 4, "h": 2}
NAMES = tuple(SIZES)
STATS = 128
MINE, OTHER = 2, 3


def permute(x, names, move):
    dims = [SIZES[n] for n in names]
    pairs = []
    for place in np.ndindex(*dims):
        target = move(dict(zip(names, place)))
        pairs.append(
            (
                int(np.ravel_multi_index(place, dims)),
                int(np.ravel_multi_index([target[n] for n in names], dims)),
            )
        )
    return lax.ppermute(x, names, pairs)


def along_z(x, step):
    def move(at):
        place = (at["h"] * 8 + at["z"] + (step if at["c"] == 0 else -step)) % 16
        return {"z": place % 8, "c": at["c"], "h": place // 8}

    return permute(x, ("z", "c", "h"), move)


def other_core(x):
    return permute(x, ("c",), lambda at: {"c": 1 - at["c"]})


def swap_y(x):
    return lax.all_to_all(x, "y", split_axis=0, concat_axis=0, tiled=True)


def pack_kernel(order, content, rotary, out, *, block):
    heads, nope = content.shape[1:]
    left = heads * nope
    width = left + rotary.shape[1]
    row = lax.broadcasted_iota(jnp.int32, (out.shape[1], STATS), 0)
    number = jnp.where(row < block, order[0], order[1]).astype(jnp.float32).astype(out.dtype)
    for i in range(out.shape[0]):
        for h in range(heads):
            out[i, :, h * nope : (h + 1) * nope] = content[:, h, :]
        out[i, :, left:width] = rotary[...]
        out[i, :, width:] = number


def pack(order, content, rotary, block, copies):
    rows, heads, nope = content.shape
    width = heads * nope + rotary.shape[1] + STATS
    vmem = pl.BlockSpec(memory_space=pltpu.VMEM)
    return pl.pallas_call(
        functools.partial(pack_kernel, block=block),
        in_specs=[pl.BlockSpec(memory_space=pltpu.SMEM), vmem, vmem],
        out_specs=vmem,
        out_shape=jax.ShapeDtypeStruct((copies, rows, width), jnp.bfloat16),
    )(order, content, rotary)


def query_kernel(start, payload, key_up, out, starts, *, heads, nope, rope):
    latent = key_up.shape[0]
    block = payload.shape[0] // starts.shape[0]
    for i in range(starts.shape[0]):
        number = payload[i * block : (i + 1) * block, payload.shape[1] - STATS :]
        starts[i] = start[0] + jnp.max(number.astype(jnp.float32)).astype(jnp.int32) * block
    for h in range(heads):
        cols = slice(h * nope, (h + 1) * nope)
        out[h, :latent, :] = lax.dot_general(
            key_up[:, cols],
            payload[:, cols],
            (((1,), (1,)), ((), ())),
            preferred_element_type=jnp.float32,
        ).astype(out.dtype)
    for p in range(heads // 2):
        cols = slice(heads * nope + 2 * p * rope, heads * nope + 2 * (p + 1) * rope)
        both = payload[:, cols].astype(jnp.float32).T.astype(out.dtype)
        out[2 * p, latent:, :] = both[:rope]
        out[2 * p + 1, latent:, :] = both[rope:]


def latent_queries(start, payload, key_up, heads, nope, rope, blocks):
    rows = payload.shape[0]
    latent = key_up.shape[0]
    smem, vmem = pl.BlockSpec(memory_space=pltpu.SMEM), pl.BlockSpec(memory_space=pltpu.VMEM)
    return pl.pallas_call(
        functools.partial(query_kernel, heads=heads, nope=nope, rope=rope),
        in_specs=[smem, vmem, vmem],
        out_specs=[vmem, smem],
        out_shape=[
            jax.ShapeDtypeStruct((heads, latent + rope, rows), jnp.bfloat16),
            jax.ShapeDtypeStruct((blocks,), jnp.int32),
        ],
        compiler_params=pltpu.CompilerParams(vmem_limit_bytes=48 * 1024 * 1024),
        cost_estimate=pl.CostEstimate(
            flops=2 * heads * rows * latent * nope, bytes_accessed=8 * 1024 * 1024, transcendentals=0
        ),
    )(start, payload, key_up)


def three_parts(x):
    parts = []
    for _ in range(3):
        part = x.astype(jnp.bfloat16).astype(jnp.float32)
        parts.append(part)
        x = x - part
    return parts


def read_stats(rows, heads):
    stats = rows[:, rows.shape[1] - STATS :].astype(jnp.float32)
    return stats[:, :heads] + stats[:, heads : 2 * heads] + stats[:, 2 * heads : 3 * heads]


def attend_kernel(
    starts, place, query, *rest, shards, coef, block, some, with_before
):
    *keys, value_up, before, out, turned, lses, olds = rest
    first = pl.program_id(0) * some
    heads, tokens = lses.shape
    value_dim, latent = value_up.shape[1:]
    width = keys[0].shape[2]
    tiles = [(r, i) for r in keys for i in range(r.shape[0])]
    columns = some * tokens
    limit = place[3]
    side = 1 - 2 * place[2]
    cores = {0: 0, 1: 1, MINE: place[2], OTHER: 1 - place[2]}
    bases = [
        ((place[0] * 8 + (place[1] + 8 - side * step) % 8) * 2 + cores[core]) * width
        for step, core in shards
    ]
    left = out.shape[1] - STATS

    @pl.when(first == 0)
    def _():
        for n, (r, i) in enumerate(tiles):
            turned[n * width : (n + 1) * width, :] = r[i].T
        if with_before:
            stats = before[:, left:].astype(jnp.float32).T
            olds[...] = stats[:heads] + stats[heads : 2 * heads] + stats[2 * heads : 3 * heads]

    highest, nearest = bases[0], starts[0]
    for i in range(1, len(shards)):
        highest = jnp.maximum(highest, bases[i])
    for i in range(1, tokens // block):
        nearest = jnp.minimum(nearest, starts[i])
    sure = highest + width - 1 <= jnp.minimum(nearest, limit - 1)

    def run(masked):
        q = jnp.concatenate([query[i] for i in range(some)], axis=1)
        s = jnp.dot(turned[...], q, preferred_element_type=jnp.float32)
        if masked:
            token = lax.broadcasted_iota(jnp.int32, (1, columns), 1) % tokens
            last = token % block
            for i in range(tokens // block):
                last = last + jnp.where(token // block == i, starts[i], 0)
            last = jnp.minimum(last, limit - 1)
            row = lax.broadcasted_iota(jnp.int32, (width, columns), 0)
            s = jnp.concatenate(
                [
                    jnp.where(row + bases[n] <= last, s[n * width : (n + 1) * width], NEG)
                    for n in range(len(shards))
                ],
                axis=0,
            )
        top = jnp.max(s, axis=0, keepdims=True)
        if masked:
            top = jnp.maximum(top, NEG / 10)
        weights = jnp.exp2(s * coef - top * coef)
        total = jnp.sum(weights, axis=0, keepdims=True)
        k = jnp.concatenate([r[i, :latent] for r, i in tiles], axis=1)
        values = jnp.dot(k, weights.astype(jnp.bfloat16), preferred_element_type=jnp.float32)
        if masked:
            seen = total > 0
            total = jnp.where(seen, total, 1.0)
            lse = jnp.where(seen, top * coef + jnp.log2(total), NEG)
        else:
            lse = top * coef + jnp.log2(total)
        mixed = (values * (1.0 / total)).astype(jnp.bfloat16)
        mine = [lse[:, i * tokens : (i + 1) * tokens] for i in range(some)]
        new = [None] * some
        if with_before:
            old = []
            for i in range(some):
                past = olds[pl.ds(first + i, 1), :]
                peak = jnp.maximum(past, mine[i])
                a, b = jnp.exp2(past - peak), jnp.exp2(mine[i] - peak)
                old.append(a / (a + b))
                new[i] = b / (a + b)
                mine[i] = peak + jnp.log2(a + b)
            old = jnp.concatenate(old + [jnp.zeros((8 - some, tokens), jnp.float32)], axis=0).T
        for i in range(some):
            lses[pl.ds(first + i, 1), :] = mine[i]
            value = jnp.dot(
                value_up[i], mixed[:, i * tokens : (i + 1) * tokens], preferred_element_type=jnp.float32
            )
            if with_before:
                value = value * new[i]
            value = value.T
            cols = pl.ds(pl.multiple_of((first + i) * value_dim, value_dim), value_dim)
            if with_before:
                value = value + before[:, cols].astype(jnp.float32) * old[:, i : i + 1]
            out[:, cols] = value.astype(out.dtype)

    @pl.when(sure)
    def _():
        run(False)

    @pl.when(jnp.logical_not(sure))
    def _():
        run(True)

    @pl.when(first + some == heads)
    def _():
        empty = jnp.zeros((STATS - 3 * heads, tokens), jnp.float32)
        stats = jnp.concatenate(three_parts(lses[...]) + [empty], axis=0)
        out[:, left:] = stats.T.astype(out.dtype)


def attend(starts, place, query, keys, shards, value_up, scale, before=None, some=4):
    heads, depth, tokens = query.shape
    value_dim, latent = value_up.shape[1:]
    width = keys[0].shape[2]
    whole = lambda shape: pl.BlockSpec(shape, lambda i, *_: (0,) * len(shape))
    kernel = functools.partial(
        attend_kernel,
        shards=shards,
        coef=scale * LOG2E,
        block=tokens // starts.shape[0],
        some=some,
        with_before=before is not None,
    )
    if before is None:
        before = jnp.zeros((16, STATS), jnp.bfloat16)
    return pl.pallas_call(
        kernel,
        grid_spec=pltpu.PrefetchScalarGridSpec(
            num_scalar_prefetch=2,
            grid=(heads // some,),
            in_specs=[pl.BlockSpec((some, depth, tokens), lambda i, *_: (i, 0, 0))]
            + [whole(k.shape) for k in keys]
            + [pl.BlockSpec((some, value_dim, latent), lambda i, *_: (i, 0, 0))]
            + [whole(before.shape)],
            out_specs=whole((tokens, heads * value_dim + STATS)),
            scratch_shapes=[
                pltpu.VMEM((len(shards) * width, depth), jnp.bfloat16),
                pltpu.VMEM((heads, tokens), jnp.float32),
                pltpu.VMEM((heads, tokens), jnp.float32),
            ],
        ),
        out_shape=jax.ShapeDtypeStruct((tokens, heads * value_dim + STATS), jnp.bfloat16),
        compiler_params=pltpu.CompilerParams(vmem_limit_bytes=48 * 1024 * 1024),
    )(starts, place, query, *keys, value_up, before)


def merge_kernel(half, parts, out, *, heads, sources):
    width = out.shape[2]
    share = out.shape[1] // 8
    first = lambda value, which: [
        value[i * share : (i + 1) * share] for i in range(8) if i % 2 == which
    ]
    each = width // heads
    lses = [read_stats(parts.at[s], heads) for s in range(sources)]
    top = functools.reduce(jnp.maximum, lses)
    weights = [jnp.exp2(v - top) for v in lses]
    total = functools.reduce(jnp.add, weights)
    weights = [w / total for w in weights]
    for h in range(heads):
        cols = slice(h * each, (h + 1) * each)
        value = functools.reduce(
            jnp.add,
            [
                weights[s][:, h : h + 1] * parts[s, :, cols].astype(jnp.float32)
                for s in range(sources)
            ],
        )
        even, odd = first(value, 0), first(value, 1)
        value = jnp.where(
            half[0] == 0, jnp.concatenate(odd + even, axis=0), jnp.concatenate(even + odd, axis=0)
        ).astype(out.dtype)
        for i in range(out.shape[0]):
            out[i, :, cols] = value


def merge(half, parts, heads, copies):
    sources, tokens, width = parts.shape
    return pl.pallas_call(
        functools.partial(merge_kernel, heads=heads, sources=sources),
        in_specs=[
            pl.BlockSpec(memory_space=pltpu.SMEM),
            pl.BlockSpec(memory_space=pltpu.VMEM),
        ],
        out_shape=jax.ShapeDtypeStruct((copies, tokens, width - STATS), jnp.bfloat16),
    )(half, parts)


def per_device(
    query_content,
    query_rotary,
    key_cache,
    key_up,
    value_up,
    output_weight,
    query_start,
    key_limit,
    block_order,
):
    tokens, heads, nope = query_content.shape
    latent = key_up.shape[0]
    rope = query_rotary.shape[1] // heads
    columns = output_weight.shape[1]
    block = tokens // 2
    scale = 1.0 / math.sqrt(nope + rope)
    y, z, c, h = (lax.axis_index(n) for n in ("y", "z", "c", "h"))

    weight = lax.all_gather(output_weight.T, "z", axis=0, tiled=True)

    packed = pack(block_order, query_content, query_rotary, block, 4)

    pair = lax.all_gather(key_cache, "c", axis=0, tiled=True).reshape(2, *key_cache.shape)
    one, two = along_z(pair, 1), along_z(pair, 2)
    key_up = key_up.reshape(latent, heads * nope)
    value_up = value_up.transpose(1, 2, 0)
    place = jnp.concatenate([jnp.stack([y, z, c]).astype(jnp.int32), key_limit])
    half = h.astype(jnp.int32)[None]
    two, _, key_up, value_up, place, half = lax.optimization_barrier(
        (two, packed, key_up, value_up, place, half)
    )
    near = jnp.concatenate([one, two], axis=0)
    near_swapped = other_core(near)
    three, four = along_z(two, 1), along_z(lax.dynamic_slice_in_dim(two, c, 1), 2)

    payload = swap_y(packed).reshape(4 * tokens, -1)
    queries, starts = latent_queries(query_start, payload, key_up, heads, nope, rope, 8)

    attend_part = functools.partial(
        attend, starts, place, queries, scale=scale, value_up=value_up
    )
    pairs = lambda steps: [(step, core) for step in steps for core in (0, 1)]
    partial = attend_part(keys=[pair, near, near_swapped], shards=pairs((0, 1, 2, -1, -2)))
    three, four, partial = lax.optimization_barrier((three, four, partial))
    partial = attend_part(
        keys=[three, other_core(three), four, other_core(four)],
        shards=pairs((3, -3)) + [(4, MINE), (4, OTHER)],
        before=partial,
    )
    values = merge(half, swap_y(partial.reshape(4, tokens, -1)), heads, 4)
    values, weight = lax.optimization_barrier((values, weight))
    weights = [weight, other_core(weight)]

    rows = swap_y(values)
    share = tokens // 8

    def summed(part):
        part = part.reshape(4 * tokens // 2, -1)
        product = jnp.concatenate(
            [
                lax.dot_general(
                    part, w, (((1,), (1,)), ((), ())), preferred_element_type=jnp.float32
                ).astype(jnp.bfloat16)
                for w in weights
            ],
            axis=1,
        )
        product = lax.all_to_all(
            product.reshape(16, share, -1), ("y", "x"), split_axis=0, concat_axis=0, tiled=True
        )
        return jnp.sum(product.reshape(4, 4, share, -1).astype(jnp.float32), axis=1)

    theirs = summed(rows[:, : tokens // 2]).astype(jnp.bfloat16)
    got = permute(theirs, ("h",), lambda at: {"h": 1 - at["h"]})
    mine = summed(rows[:, tokens // 2 :])
    total = (mine + got.astype(jnp.float32)).astype(jnp.bfloat16)
    total = total.reshape(4, share, 2, 8, columns)
    total = jnp.where(c == 0, total, total[:, :, ::-1])
    return total.transpose(1, 0, 3, 2, 4).reshape(share, 16 * 4 * columns)


def solution(mesh):
    fine = Mesh(mesh.devices.reshape(tuple(SIZES.values())), NAMES)
    seq, head = ("y", "z", "c"), ("x", "h")
    in_specs = (
        P(seq, head, None),
        P(seq, head),
        P(None, seq),
        P(None, head, None),
        P(None, head, None),
        P(head, seq),
        P(),
        P(),
        P(seq),
    )
    return jax.shard_map(
        per_device, mesh=fine, in_specs=in_specs, out_specs=P(seq + head, None), check_vma=False
    )
```

```python
import functools
import math

import jax
import jax.numpy as jnp
import numpy as np
from jax import lax
from jax.experimental import pallas as pl
from jax.experimental.pallas import tpu as pltpu
from jax.sharding import Mesh, PartitionSpec as P

NEG = -1e30
LOG2E = 1.4426950408889634
SIZES = {"y": 4, "z": 8, "c": 2, "x": 4, "h": 2}
NAMES = tuple(SIZES)
STATS = 128
MINE, OTHER = 2, 3


def permute(x, names, move):
    dims = [SIZES[n] for n in names]
    pairs = []
    for place in np.ndindex(*dims):
        target = move(dict(zip(names, place)))
        pairs.append(
            (
                int(np.ravel_multi_index(place, dims)),
                int(np.ravel_multi_index([target[n] for n in names], dims)),
            )
        )
    return lax.ppermute(x, names, pairs)


def along_z(x, step):
    def move(at):
        place = (at["h"] * 8 + at["z"] + (step if at["c"] == 0 else -step)) % 16
        return {"z": place % 8, "c": at["c"], "h": place // 8}

    return permute(x, ("z", "c", "h"), move)


def other_core(x):
    return permute(x, ("c",), lambda at: {"c": 1 - at["c"]})


def swap_y(x):
    return lax.all_to_all(x, "y", split_axis=0, concat_axis=0, tiled=True)


def pack_kernel(order, content, rotary, out, *, block):
    heads, nope = content.shape[1:]
    left = heads * nope
    width = left + rotary.shape[1]
    row = lax.broadcasted_iota(jnp.int32, (out.shape[1], STATS), 0)
    number = jnp.where(row < block, order[0], order[1]).astype(jnp.float32).astype(out.dtype)
    for i in range(out.shape[0]):
        for h in range(heads):
            out[i, :, h * nope : (h + 1) * nope] = content[:, h, :]
        out[i, :, left:width] = rotary[...]
        out[i, :, width:] = number


def pack(order, content, rotary, block, copies):
    rows, heads, nope = content.shape
    width = heads * nope + rotary.shape[1] + STATS
    vmem = pl.BlockSpec(memory_space=pltpu.VMEM)
    return pl.pallas_call(
        functools.partial(pack_kernel, block=block),
        in_specs=[pl.BlockSpec(memory_space=pltpu.SMEM), vmem, vmem],
        out_specs=vmem,
        out_shape=jax.ShapeDtypeStruct((copies, rows, width), jnp.bfloat16),
    )(order, content, rotary)


def query_kernel(start, payload, key_up, out, starts, *, heads, nope, rope):
    latent = key_up.shape[0]
    block = payload.shape[0] // starts.shape[0]
    for i in range(starts.shape[0]):
        number = payload[i * block : (i + 1) * block, payload.shape[1] - STATS :]
        starts[i] = start[0] + jnp.max(number.astype(jnp.float32)).astype(jnp.int32) * block
    for h in range(heads):
        cols = slice(h * nope, (h + 1) * nope)
        out[h, :latent, :] = lax.dot_general(
            key_up[:, cols],
            payload[:, cols],
            (((1,), (1,)), ((), ())),
            preferred_element_type=jnp.float32,
        ).astype(out.dtype)
    for p in range(heads // 2):
        cols = slice(heads * nope + 2 * p * rope, heads * nope + 2 * (p + 1) * rope)
        both = payload[:, cols].astype(jnp.float32).T.astype(out.dtype)
        out[2 * p, latent:, :] = both[:rope]
        out[2 * p + 1, latent:, :] = both[rope:]


def latent_queries(start, payload, key_up, heads, nope, rope, blocks):
    rows = payload.shape[0]
    latent = key_up.shape[0]
    smem, vmem = pl.BlockSpec(memory_space=pltpu.SMEM), pl.BlockSpec(memory_space=pltpu.VMEM)
    return pl.pallas_call(
        functools.partial(query_kernel, heads=heads, nope=nope, rope=rope),
        in_specs=[smem, vmem, vmem],
        out_specs=[vmem, smem],
        out_shape=[
            jax.ShapeDtypeStruct((heads, latent + rope, rows), jnp.bfloat16),
            jax.ShapeDtypeStruct((blocks,), jnp.int32),
        ],
        compiler_params=pltpu.CompilerParams(vmem_limit_bytes=48 * 1024 * 1024),
        cost_estimate=pl.CostEstimate(
            flops=2 * heads * rows * latent * nope, bytes_accessed=8 * 1024 * 1024, transcendentals=0
        ),
    )(start, payload, key_up)


def three_parts(x):
    parts = []
    for _ in range(3):
        part = x.astype(jnp.bfloat16).astype(jnp.float32)
        parts.append(part)
        x = x - part
    return parts


def read_stats(rows, heads):
    stats = rows[:, rows.shape[1] - STATS :].astype(jnp.float32)
    return stats[:, :heads] + stats[:, heads : 2 * heads] + stats[:, 2 * heads : 3 * heads]


def attend_kernel(
    starts, place, query, *rest, shards, coef, block, some, with_before
):
    *keys, value_up, before, out, turned, lses = rest
    heads, tokens = lses.shape
    value_dim, latent = value_up.shape[1:]
    width = keys[0].shape[2]
    tiles = [(r, i) for r in keys for i in range(r.shape[0])]
    columns = some * tokens
    limit = place[3]
    side = 1 - 2 * place[2]
    cores = {0: 0, 1: 1, MINE: place[2], OTHER: 1 - place[2]}
    bases = [
        ((place[0] * 8 + (place[1] + 8 - side * step) % 8) * 2 + cores[core]) * width
        for step, core in shards
    ]
    left = out.shape[1] - STATS

    for n, (r, i) in enumerate(tiles):
        turned[n * width : (n + 1) * width, :] = r[i].T
    if with_before:
        stats = before[:, left:].astype(jnp.float32).T
        olds = stats[:heads] + stats[heads : 2 * heads] + stats[2 * heads : 3 * heads]

    highest, nearest = bases[0], starts[0]
    for i in range(1, len(shards)):
        highest = jnp.maximum(highest, bases[i])
    for i in range(1, tokens // block):
        nearest = jnp.minimum(nearest, starts[i])
    sure = highest + width - 1 <= jnp.minimum(nearest, limit - 1)

    def run(masked, first):
        q = jnp.concatenate([query[first + i] for i in range(some)], axis=1)
        s = jnp.dot(turned[...], q, preferred_element_type=jnp.float32)
        if masked:
            token = lax.broadcasted_iota(jnp.int32, (1, columns), 1) % tokens
            last = token % block
            for i in range(tokens // block):
                last = last + jnp.where(token // block == i, starts[i], 0)
            last = jnp.minimum(last, limit - 1)
            row = lax.broadcasted_iota(jnp.int32, (width, columns), 0)
            s = jnp.concatenate(
                [
                    jnp.where(row + bases[n] <= last, s[n * width : (n + 1) * width], NEG)
                    for n in range(len(shards))
                ],
                axis=0,
            )
        top = jnp.max(s, axis=0, keepdims=True)
        if masked:
            top = jnp.maximum(top, NEG / 10)
        weights = jnp.exp2(s * coef - top * coef)
        total = jnp.sum(weights, axis=0, keepdims=True)
        k = jnp.concatenate([r[i, :latent] for r, i in tiles], axis=1)
        values = jnp.dot(k, weights.astype(jnp.bfloat16), preferred_element_type=jnp.float32)
        if masked:
            seen = total > 0
            total = jnp.where(seen, total, 1.0)
            lse = jnp.where(seen, top * coef + jnp.log2(total), NEG)
        else:
            lse = top * coef + jnp.log2(total)
        mixed = (values * (1.0 / total)).astype(jnp.bfloat16)
        mine = [lse[:, i * tokens : (i + 1) * tokens] for i in range(some)]
        new = [None] * some
        if with_before:
            old = []
            for i in range(some):
                past = olds[first + i : first + i + 1, :]
                peak = jnp.maximum(past, mine[i])
                a, b = jnp.exp2(past - peak), jnp.exp2(mine[i] - peak)
                old.append(a / (a + b))
                new[i] = b / (a + b)
                mine[i] = peak + jnp.log2(a + b)
            old = jnp.concatenate(old + [jnp.zeros((8 - some, tokens), jnp.float32)], axis=0).T
        for i in range(some):
            lses[first + i : first + i + 1, :] = mine[i]
            value = jnp.dot(
                value_up[first + i], mixed[:, i * tokens : (i + 1) * tokens], preferred_element_type=jnp.float32
            )
            if with_before:
                value = value * new[i]
            value = value.T
            cols = slice((first + i) * value_dim, (first + i + 1) * value_dim)
            if with_before:
                value = value + before[:, cols].astype(jnp.float32) * old[:, i : i + 1]
            out[:, cols] = value.astype(out.dtype)

    @pl.when(sure)
    def _():
        for first in range(0, heads, some):
            run(False, first)

    @pl.when(jnp.logical_not(sure))
    def _():
        for first in range(0, heads, some):
            run(True, first)

    empty = jnp.zeros((STATS - 3 * heads, tokens), jnp.float32)
    stats = jnp.concatenate(three_parts(lses[...]) + [empty], axis=0)
    out[:, left:] = stats.T.astype(out.dtype)


def attend(starts, place, query, keys, shards, value_up, scale, before=None, some=4):
    heads, depth, tokens = query.shape
    value_dim, latent = value_up.shape[1:]
    width = keys[0].shape[2]
    kernel = functools.partial(
        attend_kernel,
        shards=shards,
        coef=scale * LOG2E,
        block=tokens // starts.shape[0],
        some=some,
        with_before=before is not None,
    )
    if before is None:
        before = jnp.zeros((16, STATS), jnp.bfloat16)
    return pl.pallas_call(
        kernel,
        in_specs=[pl.BlockSpec(memory_space=pltpu.SMEM)] * 2
        + [pl.BlockSpec(memory_space=pltpu.VMEM)] * (len(keys) + 3),
        out_specs=pl.BlockSpec(memory_space=pltpu.VMEM),
        scratch_shapes=[
            pltpu.VMEM((len(shards) * width, depth), jnp.bfloat16),
            pltpu.VMEM((heads, tokens), jnp.float32),
        ],
        out_shape=jax.ShapeDtypeStruct((tokens, heads * value_dim + STATS), jnp.bfloat16),
        compiler_params=pltpu.CompilerParams(vmem_limit_bytes=40 * 1024 * 1024),
    )(starts, place, query, *keys, value_up, before)


def merge_kernel(half, parts, out, *, heads, sources):
    width = out.shape[2]
    share = out.shape[1] // 8
    first = lambda value, which: [
        value[i * share : (i + 1) * share] for i in range(8) if i % 2 == which
    ]
    each = width // heads
    lses = [read_stats(parts.at[s], heads) for s in range(sources)]
    top = functools.reduce(jnp.maximum, lses)
    weights = [jnp.exp2(v - top) for v in lses]
    total = functools.reduce(jnp.add, weights)
    weights = [w / total for w in weights]
    for h in range(heads):
        cols = slice(h * each, (h + 1) * each)
        value = functools.reduce(
            jnp.add,
            [
                weights[s][:, h : h + 1] * parts[s, :, cols].astype(jnp.float32)
                for s in range(sources)
            ],
        )
        even, odd = first(value, 0), first(value, 1)
        value = jnp.where(
            half[0] == 0, jnp.concatenate(odd + even, axis=0), jnp.concatenate(even + odd, axis=0)
        ).astype(out.dtype)
        for i in range(out.shape[0]):
            out[i, :, cols] = value


def merge(half, parts, heads, copies):
    sources, tokens, width = parts.shape
    return pl.pallas_call(
        functools.partial(merge_kernel, heads=heads, sources=sources),
        in_specs=[
            pl.BlockSpec(memory_space=pltpu.SMEM),
            pl.BlockSpec(memory_space=pltpu.VMEM),
        ],
        out_shape=jax.ShapeDtypeStruct((copies, tokens, width - STATS), jnp.bfloat16),
    )(half, parts)


def per_device(
    query_content,
    query_rotary,
    key_cache,
    key_up,
    value_up,
    output_weight,
    query_start,
    key_limit,
    block_order,
):
    tokens, heads, nope = query_content.shape
    latent = key_up.shape[0]
    rope = query_rotary.shape[1] // heads
    columns = output_weight.shape[1]
    block = tokens // 2
    scale = 1.0 / math.sqrt(nope + rope)
    y, z, c, h = (lax.axis_index(n) for n in ("y", "z", "c", "h"))

    weight = lax.all_gather(output_weight.T, "z", axis=0, tiled=True)

    packed = pack(block_order, query_content, query_rotary, block, 4)

    pair = lax.all_gather(key_cache, "c", axis=0, tiled=True).reshape(2, *key_cache.shape)
    one, two = along_z(pair, 1), along_z(pair, 2)
    key_up = key_up.reshape(latent, heads * nope)
    value_up = value_up.transpose(1, 2, 0)
    place = jnp.concatenate([jnp.stack([y, z, c]).astype(jnp.int32), key_limit])
    half = h.astype(jnp.int32)[None]
    two, _, key_up, value_up, place, half = lax.optimization_barrier(
        (two, packed, key_up, value_up, place, half)
    )
    near = jnp.concatenate([one, two], axis=0)
    near_swapped = other_core(near)
    three, four = along_z(two, 1), along_z(lax.dynamic_slice_in_dim(two, c, 1), 2)

    payload = swap_y(packed).reshape(4 * tokens, -1)
    queries, starts = latent_queries(query_start, payload, key_up, heads, nope, rope, 8)

    attend_part = functools.partial(
        attend, starts, place, queries, scale=scale, value_up=value_up
    )
    pairs = lambda steps: [(step, core) for step in steps for core in (0, 1)]
    partial = attend_part(
        keys=[pair, near, near_swapped], shards=pairs((0, 1, 2, -1, -2))
    )
    three, four, partial = lax.optimization_barrier((three, four, partial))
    partial = attend_part(
        keys=[three, other_core(three), four, other_core(four)],
        shards=pairs((3, -3)) + [(4, MINE), (4, OTHER)],
        before=partial,
    )
    values = merge(half, swap_y(partial.reshape(4, tokens, -1)), heads, 4)
    values, weight = lax.optimization_barrier((values, weight))
    weights = [weight, other_core(weight)]

    rows = swap_y(values)
    share = tokens // 8

    def summed(part):
        part = part.reshape(4 * tokens // 2, -1)
        product = jnp.concatenate(
            [
                lax.dot_general(
                    part, w, (((1,), (1,)), ((), ())), preferred_element_type=jnp.float32
                ).astype(jnp.bfloat16)
                for w in weights
            ],
            axis=1,
        )
        product = lax.all_to_all(
            product.reshape(16, share, -1), ("y", "x"), split_axis=0, concat_axis=0, tiled=True
        )
        return jnp.sum(product.reshape(4, 4, share, -1).astype(jnp.float32), axis=1)

    theirs = summed(rows[:, : tokens // 2]).astype(jnp.bfloat16)
    got = permute(theirs, ("h",), lambda at: {"h": 1 - at["h"]})
    mine = summed(rows[:, tokens // 2 :])
    total = (mine + got.astype(jnp.float32)).astype(jnp.bfloat16)
    total = total.reshape(4, share, 2, 8, columns)
    total = jnp.where(c == 0, total, total[:, :, ::-1])
    return total.transpose(1, 0, 3, 2, 4).reshape(share, 16 * 4 * columns)


def solution(mesh):
    fine = Mesh(mesh.devices.reshape(tuple(SIZES.values())), NAMES)
    seq, head = ("y", "z", "c"), ("x", "h")
    in_specs = (
        P(seq, head, None),
        P(seq, head),
        P(None, seq),
        P(None, head, None),
        P(None, head, None),
        P(head, seq),
        P(),
        P(),
        P(seq),
    )
    return jax.shard_map(
        per_device, mesh=fine, in_specs=in_specs, out_specs=P(seq + head, None), check_vma=False
    )
```

```python
import functools
import math

import jax
import jax.numpy as jnp
import numpy as np
from jax import lax
from jax.experimental import pallas as pl
from jax.experimental.pallas import tpu as pltpu
from jax.sharding import Mesh, PartitionSpec as P

NEG = -1e30
LOG2E = 1.4426950408889634
SIZES = {"y": 4, "z": 8, "c": 2, "x": 4, "h": 2}
NAMES = tuple(SIZES)
STATS = 128
MINE, OTHER = 2, 3


def permute(x, names, move):
    dims = [SIZES[n] for n in names]
    pairs = []
    for place in np.ndindex(*dims):
        target = move(dict(zip(names, place)))
        pairs.append(
            (
                int(np.ravel_multi_index(place, dims)),
                int(np.ravel_multi_index([target[n] for n in names], dims)),
            )
        )
    return lax.ppermute(x, names, pairs)


def along_z(x, step):
    def move(at):
        place = (at["h"] * 8 + at["z"] + (step if at["c"] == 0 else -step)) % 16
        return {"z": place % 8, "c": at["c"], "h": place // 8}

    return permute(x, ("z", "c", "h"), move)


def other_core(x):
    return permute(x, ("c",), lambda at: {"c": 1 - at["c"]})


def swap_y(x):
    return lax.all_to_all(x, "y", split_axis=0, concat_axis=0, tiled=True)


def pack_kernel(order, content, rotary, out, *, block):
    heads, nope = content.shape[1:]
    left = heads * nope
    width = left + rotary.shape[1]
    row = lax.broadcasted_iota(jnp.int32, (out.shape[1], STATS), 0)
    number = jnp.where(row < block, order[0], order[1]).astype(jnp.float32).astype(out.dtype)
    for i in range(out.shape[0]):
        for h in range(heads):
            out[i, :, h * nope : (h + 1) * nope] = content[:, h, :]
        out[i, :, left:width] = rotary[...]
        out[i, :, width:] = number


def pack(order, content, rotary, block, copies):
    rows, heads, nope = content.shape
    width = heads * nope + rotary.shape[1] + STATS
    vmem = pl.BlockSpec(memory_space=pltpu.VMEM)
    return pl.pallas_call(
        functools.partial(pack_kernel, block=block),
        in_specs=[pl.BlockSpec(memory_space=pltpu.SMEM), vmem, vmem],
        out_specs=vmem,
        out_shape=jax.ShapeDtypeStruct((copies, rows, width), jnp.bfloat16),
    )(order, content, rotary)


def query_kernel(start, payload, key_up, out, starts, *, heads, nope, rope):
    latent = key_up.shape[0]
    block = payload.shape[0] // starts.shape[0]
    for i in range(starts.shape[0]):
        number = payload[i * block : (i + 1) * block, payload.shape[1] - STATS :]
        starts[i] = start[0] + jnp.max(number.astype(jnp.float32)).astype(jnp.int32) * block
    for h in range(heads):
        cols = slice(h * nope, (h + 1) * nope)
        out[h, :latent, :] = lax.dot_general(
            key_up[:, cols],
            payload[:, cols],
            (((1,), (1,)), ((), ())),
            preferred_element_type=jnp.float32,
        ).astype(out.dtype)
    for p in range(heads // 2):
        cols = slice(heads * nope + 2 * p * rope, heads * nope + 2 * (p + 1) * rope)
        both = payload[:, cols].astype(jnp.float32).T.astype(out.dtype)
        out[2 * p, latent:, :] = both[:rope]
        out[2 * p + 1, latent:, :] = both[rope:]


def latent_queries(start, payload, key_up, heads, nope, rope, blocks):
    rows = payload.shape[0]
    latent = key_up.shape[0]
    smem, vmem = pl.BlockSpec(memory_space=pltpu.SMEM), pl.BlockSpec(memory_space=pltpu.VMEM)
    return pl.pallas_call(
        functools.partial(query_kernel, heads=heads, nope=nope, rope=rope),
        in_specs=[smem, vmem, vmem],
        out_specs=[vmem, smem],
        out_shape=[
            jax.ShapeDtypeStruct((heads, latent + rope, rows), jnp.bfloat16),
            jax.ShapeDtypeStruct((blocks,), jnp.int32),
        ],
        compiler_params=pltpu.CompilerParams(vmem_limit_bytes=48 * 1024 * 1024),
        cost_estimate=pl.CostEstimate(
            flops=2 * heads * rows * latent * nope, bytes_accessed=8 * 1024 * 1024, transcendentals=0
        ),
    )(start, payload, key_up)


def three_parts(x):
    parts = []
    for _ in range(3):
        part = x.astype(jnp.bfloat16).astype(jnp.float32)
        parts.append(part)
        x = x - part
    return parts


def read_stats(rows, heads):
    stats = rows[:, rows.shape[1] - STATS :].astype(jnp.float32)
    return stats[:, :heads] + stats[:, heads : 2 * heads] + stats[:, 2 * heads : 3 * heads]


def attend_kernel(
    starts, place, query, *rest, shards, coef, block, some, with_before
):
    *keys, value_up, before, out, turned, lses = rest
    heads, tokens = lses.shape
    value_dim, latent = value_up.shape[1:]
    width = keys[0].shape[2]
    tiles = [(r, i) for r in keys for i in range(r.shape[0])]
    columns = some * tokens
    limit = place[3]
    side = 1 - 2 * place[2]
    cores = {0: 0, 1: 1, MINE: place[2], OTHER: 1 - place[2]}
    bases = [
        ((place[0] * 8 + (place[1] + 8 - side * step) % 8) * 2 + cores[core]) * width
        for step, core in shards
    ]
    left = out.shape[1] - STATS

    for n, (r, i) in enumerate(tiles):
        turned[n * width : (n + 1) * width, :] = r[i].T
    if with_before:
        stats = before[:, left:].astype(jnp.float32).T
        olds = stats[:heads] + stats[heads : 2 * heads] + stats[2 * heads : 3 * heads]

    highest, nearest = bases[0], starts[0]
    for i in range(1, len(shards)):
        highest = jnp.maximum(highest, bases[i])
    for i in range(1, tokens // block):
        nearest = jnp.minimum(nearest, starts[i])
    sure = highest + width - 1 <= jnp.minimum(nearest, limit - 1)

    def run(masked, first):
        q = jnp.concatenate([query[first + i] for i in range(some)], axis=1)
        s = jnp.dot(turned[...], q, preferred_element_type=jnp.float32)
        if masked:
            token = lax.broadcasted_iota(jnp.int32, (1, columns), 1) % tokens
            last = token % block
            for i in range(tokens // block):
                last = last + jnp.where(token // block == i, starts[i], 0)
            last = jnp.minimum(last, limit - 1)
            row = lax.broadcasted_iota(jnp.int32, (width, columns), 0)
            s = jnp.concatenate(
                [
                    jnp.where(row + bases[n] <= last, s[n * width : (n + 1) * width], NEG)
                    for n in range(len(shards))
                ],
                axis=0,
            )
        top = jnp.max(s, axis=0, keepdims=True)
        if masked:
            top = jnp.maximum(top, NEG / 10)
        weights = jnp.exp2(s * coef - top * coef)
        total = jnp.sum(weights, axis=0, keepdims=True)
        k = jnp.concatenate([r[i, :latent] for r, i in tiles], axis=1)
        values = jnp.dot(k, weights.astype(jnp.bfloat16), preferred_element_type=jnp.float32)
        if masked:
            seen = total > 0
            total = jnp.where(seen, total, 1.0)
            lse = jnp.where(seen, top * coef + jnp.log2(total), NEG)
        else:
            lse = top * coef + jnp.log2(total)
        mixed = (values * (1.0 / total)).astype(jnp.bfloat16)
        mine = [lse[:, i * tokens : (i + 1) * tokens] for i in range(some)]
        new = [None] * some
        if with_before:
            old = []
            for i in range(some):
                past = olds[first + i : first + i + 1, :]
                peak = jnp.maximum(past, mine[i])
                a, b = jnp.exp2(past - peak), jnp.exp2(mine[i] - peak)
                old.append(a / (a + b))
                new[i] = b / (a + b)
                mine[i] = peak + jnp.log2(a + b)
            old = jnp.concatenate(old + [jnp.zeros((8 - some, tokens), jnp.float32)], axis=0).T
        for i in range(some):
            lses[first + i : first + i + 1, :] = mine[i]
            value = jnp.dot(
                value_up[first + i], mixed[:, i * tokens : (i + 1) * tokens], preferred_element_type=jnp.float32
            )
            if with_before:
                value = value * new[i]
            value = value.T
            cols = slice((first + i) * value_dim, (first + i + 1) * value_dim)
            if with_before:
                value = value + before[:, cols].astype(jnp.float32) * old[:, i : i + 1]
            out[:, cols] = value.astype(out.dtype)

    @pl.when(sure)
    def _():
        for first in range(0, heads, some):
            run(False, first)

    @pl.when(jnp.logical_not(sure))
    def _():
        for first in range(0, heads, some):
            run(True, first)

    empty = jnp.zeros((STATS - 3 * heads, tokens), jnp.float32)
    stats = jnp.concatenate(three_parts(lses[...]) + [empty], axis=0)
    out[:, left:] = stats.T.astype(out.dtype)


def attend(starts, place, query, keys, shards, value_up, scale, before=None, some=4):
    heads, depth, tokens = query.shape
    value_dim, latent = value_up.shape[1:]
    width = keys[0].shape[2]
    kernel = functools.partial(
        attend_kernel,
        shards=shards,
        coef=scale * LOG2E,
        block=tokens // starts.shape[0],
        some=some,
        with_before=before is not None,
    )
    if before is None:
        before = jnp.zeros((16, STATS), jnp.bfloat16)
    return pl.pallas_call(
        kernel,
        in_specs=[pl.BlockSpec(memory_space=pltpu.SMEM)] * 2
        + [pl.BlockSpec(memory_space=pltpu.VMEM)] * (len(keys) + 3),
        out_specs=pl.BlockSpec(memory_space=pltpu.VMEM),
        scratch_shapes=[
            pltpu.VMEM((len(shards) * width, depth), jnp.bfloat16),
            pltpu.VMEM((heads, tokens), jnp.float32),
        ],
        out_shape=jax.ShapeDtypeStruct((tokens, heads * value_dim + STATS), jnp.bfloat16),
        compiler_params=pltpu.CompilerParams(vmem_limit_bytes=40 * 1024 * 1024),
    )(starts, place, query, *keys, value_up, before)


def merge_kernel(half, parts, out, *, heads, sources):
    width = out.shape[2]
    share = out.shape[1] // 8
    first = lambda value, which: [
        value[i * share : (i + 1) * share] for i in range(8) if i % 2 == which
    ]
    each = width // heads
    lses = [read_stats(parts.at[s], heads) for s in range(sources)]
    top = functools.reduce(jnp.maximum, lses)
    weights = [jnp.exp2(v - top) for v in lses]
    total = functools.reduce(jnp.add, weights)
    weights = [w / total for w in weights]
    for h in range(heads):
        cols = slice(h * each, (h + 1) * each)
        value = functools.reduce(
            jnp.add,
            [
                weights[s][:, h : h + 1] * parts[s, :, cols].astype(jnp.float32)
                for s in range(sources)
            ],
        )
        even, odd = first(value, 0), first(value, 1)
        value = jnp.where(
            half[0] == 0, jnp.concatenate(odd + even, axis=0), jnp.concatenate(even + odd, axis=0)
        ).astype(out.dtype)
        for i in range(out.shape[0]):
            out[i, :, cols] = value


def merge(half, parts, heads, copies):
    sources, tokens, width = parts.shape
    return pl.pallas_call(
        functools.partial(merge_kernel, heads=heads, sources=sources),
        in_specs=[
            pl.BlockSpec(memory_space=pltpu.SMEM),
            pl.BlockSpec(memory_space=pltpu.VMEM),
        ],
        out_shape=jax.ShapeDtypeStruct((copies, tokens, width - STATS), jnp.bfloat16),
    )(half, parts)


def per_device(
    query_content,
    query_rotary,
    key_cache,
    key_up,
    value_up,
    output_weight,
    query_start,
    key_limit,
    block_order,
):
    tokens, heads, nope = query_content.shape
    latent = key_up.shape[0]
    rope = query_rotary.shape[1] // heads
    columns = output_weight.shape[1]
    block = tokens // 2
    scale = 1.0 / math.sqrt(nope + rope)
    y, z, c, h = (lax.axis_index(n) for n in ("y", "z", "c", "h"))

    weight = lax.all_gather(output_weight.T, "z", axis=0, tiled=True)

    packed = pack(block_order, query_content, query_rotary, block, 4)

    pair = lax.all_gather(key_cache, "c", axis=0, tiled=True).reshape(2, *key_cache.shape)
    one, two = along_z(pair, 1), along_z(pair, 2)
    key_up = key_up.reshape(latent, heads * nope)
    value_up = value_up.transpose(1, 2, 0)
    place = jnp.concatenate([jnp.stack([y, z, c]).astype(jnp.int32), key_limit])
    half = h.astype(jnp.int32)[None]
    two, _, key_up, value_up, place, half = lax.optimization_barrier(
        (two, packed, key_up, value_up, place, half)
    )
    own = lax.dynamic_slice_in_dim(two, c, 1)
    three = along_z(two, 1)
    own, one, near_two = lax.optimization_barrier((own, one, two))
    four = along_z(own, 2)
    near = jnp.concatenate([one, near_two], axis=0)
    near_swapped = other_core(near)

    payload = swap_y(packed).reshape(4 * tokens, -1)
    queries, starts = latent_queries(query_start, payload, key_up, heads, nope, rope, 8)

    attend_part = functools.partial(
        attend, starts, place, queries, scale=scale, value_up=value_up
    )
    pairs = lambda steps: [(step, core) for step in steps for core in (0, 1)]
    partial = attend_part(
        keys=[pair, near, near_swapped], shards=pairs((0, 1, 2, -1, -2))
    )
    three, four, partial = lax.optimization_barrier((three, four, partial))
    partial = attend_part(
        keys=[three, other_core(three), four, other_core(four)],
        shards=pairs((3, -3)) + [(4, MINE), (4, OTHER)],
        before=partial,
    )
    values = merge(half, swap_y(partial.reshape(4, tokens, -1)), heads, 4)
    values, weight = lax.optimization_barrier((values, weight))
    weights = [weight, other_core(weight)]

    rows = swap_y(values)
    share = tokens // 8

    def summed(part):
        part = part.reshape(4 * tokens // 2, -1)
        product = jnp.concatenate(
            [
                lax.dot_general(
                    part, w, (((1,), (1,)), ((), ())), preferred_element_type=jnp.float32
                ).astype(jnp.bfloat16)
                for w in weights
            ],
            axis=1,
        )
        product = lax.all_to_all(
            product.reshape(16, share, -1), ("y", "x"), split_axis=0, concat_axis=0, tiled=True
        )
        return jnp.sum(product.reshape(4, 4, share, -1).astype(jnp.float32), axis=1)

    theirs = summed(rows[:, : tokens // 2]).astype(jnp.bfloat16)
    got = permute(theirs, ("h",), lambda at: {"h": 1 - at["h"]})
    mine = summed(rows[:, tokens // 2 :])
    total = (mine + got.astype(jnp.float32)).astype(jnp.bfloat16)
    total = total.reshape(4, share, 2, 8, columns)
    total = jnp.where(c == 0, total, total[:, :, ::-1])
    return total.transpose(1, 0, 3, 2, 4).reshape(share, 16 * 4 * columns)


def solution(mesh):
    fine = Mesh(mesh.devices.reshape(tuple(SIZES.values())), NAMES)
    seq, head = ("y", "z", "c"), ("x", "h")
    in_specs = (
        P(seq, head, None),
        P(seq, head),
        P(None, seq),
        P(None, head, None),
        P(None, head, None),
        P(head, seq),
        P(),
        P(),
        P(seq),
    )
    return jax.shard_map(
        per_device, mesh=fine, in_specs=in_specs, out_specs=P(seq + head, None), check_vma=False
    )
```

```python
import functools
import math

import jax
import jax.numpy as jnp
import numpy as np
from jax import lax
from jax.experimental import pallas as pl
from jax.experimental.pallas import tpu as pltpu
from jax.sharding import Mesh, PartitionSpec as P

NEG = -1e30
LOG2E = 1.4426950408889634
SIZES = {"y": 4, "z": 8, "c": 2, "x": 4, "h": 2}
NAMES = tuple(SIZES)
RING = (0, 2, 4, 6, 7, 5, 3, 1)
STATS = 128
MINE, OTHER = 2, 3


def permute(x, names, move):
    dims = [SIZES[n] for n in names]
    pairs = []
    for place in np.ndindex(*dims):
        target = move(dict(zip(names, place)))
        pairs.append(
            (
                int(np.ravel_multi_index(place, dims)),
                int(np.ravel_multi_index([target[n] for n in names], dims)),
            )
        )
    return lax.ppermute(x, names, pairs)


def along_z(x, step):
    def move(at):
        place = (at["h"] * 8 + at["z"] + (step if at["c"] == 0 else -step)) % 16
        return {"z": place % 8, "c": at["c"], "h": place // 8}

    return permute(x, ("z", "c", "h"), move)


def other_core(x):
    return permute(x, ("c",), lambda at: {"c": 1 - at["c"]})


def swap_y(x):
    return lax.all_to_all(x, "y", split_axis=0, concat_axis=0, tiled=True)


def pack_kernel(order, content, rotary, out, *, block):
    heads, nope = content.shape[1:]
    left = heads * nope
    width = left + rotary.shape[1]
    row = lax.broadcasted_iota(jnp.int32, (out.shape[1], STATS), 0)
    number = jnp.where(row < block, order[0], order[1]).astype(jnp.float32).astype(out.dtype)
    for i in range(out.shape[0]):
        for h in range(heads):
            out[i, :, h * nope : (h + 1) * nope] = content[:, h, :]
        out[i, :, left:width] = rotary[...]
        out[i, :, width:] = number


def pack(order, content, rotary, block, copies):
    rows, heads, nope = content.shape
    width = heads * nope + rotary.shape[1] + STATS
    vmem = pl.BlockSpec(memory_space=pltpu.VMEM)
    return pl.pallas_call(
        functools.partial(pack_kernel, block=block),
        in_specs=[pl.BlockSpec(memory_space=pltpu.SMEM), vmem, vmem],
        out_specs=vmem,
        out_shape=jax.ShapeDtypeStruct((copies, rows, width), jnp.bfloat16),
    )(order, content, rotary)


def query_kernel(start, payload, key_up, out, starts, *, heads, nope, rope):
    latent = key_up.shape[0]
    block = payload.shape[0] // starts.shape[0]
    for i in range(starts.shape[0]):
        number = payload[i * block : (i + 1) * block, payload.shape[1] - STATS :]
        starts[i] = start[0] + jnp.max(number.astype(jnp.float32)).astype(jnp.int32) * block
    for h in range(heads):
        cols = slice(h * nope, (h + 1) * nope)
        out[h, :latent, :] = lax.dot_general(
            key_up[:, cols],
            payload[:, cols],
            (((1,), (1,)), ((), ())),
            preferred_element_type=jnp.float32,
        ).astype(out.dtype)
    for p in range(heads // 2):
        cols = slice(heads * nope + 2 * p * rope, heads * nope + 2 * (p + 1) * rope)
        both = payload[:, cols].astype(jnp.float32).T.astype(out.dtype)
        out[2 * p, latent:, :] = both[:rope]
        out[2 * p + 1, latent:, :] = both[rope:]


def latent_queries(start, payload, key_up, heads, nope, rope, blocks):
    rows = payload.shape[0]
    latent = key_up.shape[0]
    smem, vmem = pl.BlockSpec(memory_space=pltpu.SMEM), pl.BlockSpec(memory_space=pltpu.VMEM)
    return pl.pallas_call(
        functools.partial(query_kernel, heads=heads, nope=nope, rope=rope),
        in_specs=[smem, vmem, vmem],
        out_specs=[vmem, smem],
        out_shape=[
            jax.ShapeDtypeStruct((heads, latent + rope, rows), jnp.bfloat16),
            jax.ShapeDtypeStruct((blocks,), jnp.int32),
        ],
        compiler_params=pltpu.CompilerParams(vmem_limit_bytes=48 * 1024 * 1024),
        cost_estimate=pl.CostEstimate(
            flops=2 * heads * rows * latent * nope, bytes_accessed=8 * 1024 * 1024, transcendentals=0
        ),
    )(start, payload, key_up)


def three_parts(x):
    parts = []
    for _ in range(3):
        part = x.astype(jnp.bfloat16).astype(jnp.float32)
        parts.append(part)
        x = x - part
    return parts


def read_stats(rows, heads):
    stats = rows[:, rows.shape[1] - STATS :].astype(jnp.float32)
    return stats[:, :heads] + stats[:, heads : 2 * heads] + stats[:, 2 * heads : 3 * heads]


def attend_kernel(
    starts, place, query, *rest, shards, coef, block, some, with_before
):
    *keys, value_up, before, out, turned, lses = rest
    heads, tokens = lses.shape
    value_dim, latent = value_up.shape[1:]
    width = keys[0].shape[2]
    tiles = [(r, i) for r in keys for i in range(r.shape[0])]
    columns = some * tokens
    limit = place[3]
    side = 1 - 2 * place[2]
    cores = {0: 0, 1: 1, MINE: place[2], OTHER: 1 - place[2]}
    bases = [
        ((place[0] * 8 + (place[1] + 8 - side * step) % 8) * 2 + cores[core]) * width
        for step, core in shards
    ]
    left = out.shape[1] - STATS

    for n, (r, i) in enumerate(tiles):
        turned[n * width : (n + 1) * width, :] = r[i].T
    if with_before:
        stats = before[:, left:].astype(jnp.float32).T
        olds = stats[:heads] + stats[heads : 2 * heads] + stats[2 * heads : 3 * heads]

    highest, nearest = bases[0], starts[0]
    for i in range(1, len(shards)):
        highest = jnp.maximum(highest, bases[i])
    for i in range(1, tokens // block):
        nearest = jnp.minimum(nearest, starts[i])
    sure = highest + width - 1 <= jnp.minimum(nearest, limit - 1)

    def run(masked, first):
        q = jnp.concatenate([query[first + i] for i in range(some)], axis=1)
        s = jnp.dot(turned[...], q, preferred_element_type=jnp.float32)
        if masked:
            token = lax.broadcasted_iota(jnp.int32, (1, columns), 1) % tokens
            last = token % block
            for i in range(tokens // block):
                last = last + jnp.where(token // block == i, starts[i], 0)
            last = jnp.minimum(last, limit - 1)
            row = lax.broadcasted_iota(jnp.int32, (width, columns), 0)
            s = jnp.concatenate(
                [
                    jnp.where(row + bases[n] <= last, s[n * width : (n + 1) * width], NEG)
                    for n in range(len(shards))
                ],
                axis=0,
            )
        top = jnp.max(s, axis=0, keepdims=True)
        if masked:
            top = jnp.maximum(top, NEG / 10)
        weights = jnp.exp2(s * coef - top * coef)
        total = jnp.sum(weights, axis=0, keepdims=True)
        k = jnp.concatenate([r[i, :latent] for r, i in tiles], axis=1)
        values = jnp.dot(k, weights.astype(jnp.bfloat16), preferred_element_type=jnp.float32)
        if masked:
            seen = total > 0
            total = jnp.where(seen, total, 1.0)
            lse = jnp.where(seen, top * coef + jnp.log2(total), NEG)
        else:
            lse = top * coef + jnp.log2(total)
        mixed = (values * (1.0 / total)).astype(jnp.bfloat16)
        mine = [lse[:, i * tokens : (i + 1) * tokens] for i in range(some)]
        new = [None] * some
        if with_before:
            old = []
            for i in range(some):
                past = olds[first + i : first + i + 1, :]
                peak = jnp.maximum(past, mine[i])
                a, b = jnp.exp2(past - peak), jnp.exp2(mine[i] - peak)
                old.append(a / (a + b))
                new[i] = b / (a + b)
                mine[i] = peak + jnp.log2(a + b)
            old = jnp.concatenate(old + [jnp.zeros((8 - some, tokens), jnp.float32)], axis=0).T
        for i in range(some):
            lses[first + i : first + i + 1, :] = mine[i]
            value = jnp.dot(
                value_up[first + i], mixed[:, i * tokens : (i + 1) * tokens], preferred_element_type=jnp.float32
            )
            if with_before:
                value = value * new[i]
            value = value.T
            cols = slice((first + i) * value_dim, (first + i + 1) * value_dim)
            if with_before:
                value = value + before[:, cols].astype(jnp.float32) * old[:, i : i + 1]
            out[:, cols] = value.astype(out.dtype)

    @pl.when(sure)
    def _():
        for first in range(0, heads, some):
            run(False, first)

    @pl.when(jnp.logical_not(sure))
    def _():
        for first in range(0, heads, some):
            run(True, first)

    empty = jnp.zeros((STATS - 3 * heads, tokens), jnp.float32)
    stats = jnp.concatenate(three_parts(lses[...]) + [empty], axis=0)
    out[:, left:] = stats.T.astype(out.dtype)


def attend(starts, place, query, keys, shards, value_up, scale, before=None, some=4):
    heads, depth, tokens = query.shape
    value_dim, latent = value_up.shape[1:]
    width = keys[0].shape[2]
    kernel = functools.partial(
        attend_kernel,
        shards=shards,
        coef=scale * LOG2E,
        block=tokens // starts.shape[0],
        some=some,
        with_before=before is not None,
    )
    if before is None:
        before = jnp.zeros((16, STATS), jnp.bfloat16)
    return pl.pallas_call(
        kernel,
        in_specs=[pl.BlockSpec(memory_space=pltpu.SMEM)] * 2
        + [pl.BlockSpec(memory_space=pltpu.VMEM)] * (len(keys) + 3),
        out_specs=pl.BlockSpec(memory_space=pltpu.VMEM),
        scratch_shapes=[
            pltpu.VMEM((len(shards) * width, depth), jnp.bfloat16),
            pltpu.VMEM((heads, tokens), jnp.float32),
        ],
        out_shape=jax.ShapeDtypeStruct((tokens, heads * value_dim + STATS), jnp.bfloat16),
        compiler_params=pltpu.CompilerParams(vmem_limit_bytes=40 * 1024 * 1024),
    )(starts, place, query, *keys, value_up, before)


def merge_kernel(half, parts, out, *, heads, sources):
    width = out.shape[2]
    share = out.shape[1] // 8
    first = lambda value, which: [
        value[i * share : (i + 1) * share] for i in range(8) if i % 2 == which
    ]
    each = width // heads
    lses = [read_stats(parts.at[s], heads) for s in range(sources)]
    top = functools.reduce(jnp.maximum, lses)
    weights = [jnp.exp2(v - top) for v in lses]
    total = functools.reduce(jnp.add, weights)
    weights = [w / total for w in weights]
    for h in range(heads):
        cols = slice(h * each, (h + 1) * each)
        value = functools.reduce(
            jnp.add,
            [
                weights[s][:, h : h + 1] * parts[s, :, cols].astype(jnp.float32)
                for s in range(sources)
            ],
        )
        even, odd = first(value, 0), first(value, 1)
        value = jnp.where(
            half[0] == 0, jnp.concatenate(odd + even, axis=0), jnp.concatenate(even + odd, axis=0)
        ).astype(out.dtype)
        for i in range(out.shape[0]):
            out[i, :, cols] = value


def merge(half, parts, heads, copies):
    sources, tokens, width = parts.shape
    return pl.pallas_call(
        functools.partial(merge_kernel, heads=heads, sources=sources),
        in_specs=[
            pl.BlockSpec(memory_space=pltpu.SMEM),
            pl.BlockSpec(memory_space=pltpu.VMEM),
        ],
        out_shape=jax.ShapeDtypeStruct((copies, tokens, width - STATS), jnp.bfloat16),
    )(half, parts)


def assemble_kernel(core, mine, got, out, *, columns):
    ring = len(RING)
    for y in range(mine.shape[0]):
        total = mine[y] + got[y].astype(jnp.float32)
        own, other = total[:, : ring * columns], total[:, ring * columns :]
        cores = [jnp.where(core[0] == n, own, other) for n in (0, 1)]
        pieces = []
        for z in range(ring):
            at = RING.index(z) * columns
            pieces += [cores[n][:, at : at + columns] for n in (0, 1)]
        row = jnp.concatenate(pieces, axis=1)
        out[:, y * row.shape[1] : (y + 1) * row.shape[1]] = row.astype(out.dtype)


def assemble(core, mine, got, columns):
    count, share, width = mine.shape
    return pl.pallas_call(
        functools.partial(assemble_kernel, columns=columns),
        in_specs=[
            pl.BlockSpec(memory_space=pltpu.SMEM),
            pl.BlockSpec(memory_space=pltpu.VMEM),
            pl.BlockSpec(memory_space=pltpu.VMEM),
        ],
        out_specs=pl.BlockSpec(memory_space=pltpu.VMEM),
        out_shape=jax.ShapeDtypeStruct((share, count * width), jnp.bfloat16),
    )(core, mine, got)


def per_device(
    query_content,
    query_rotary,
    key_cache,
    key_up,
    value_up,
    output_weight,
    query_start,
    key_limit,
    block_order,
):
    tokens, heads, nope = query_content.shape
    latent = key_up.shape[0]
    rope = query_rotary.shape[1] // heads
    columns = output_weight.shape[1]
    block = tokens // 2
    scale = 1.0 / math.sqrt(nope + rope)
    y, z, c, h = (lax.axis_index(n) for n in ("y", "z", "c", "h"))

    weight = lax.all_gather(
        output_weight.T, "z", axis=0, tiled=True, axis_index_groups=[list(RING)]
    )

    packed = pack(block_order, query_content, query_rotary, block, 4)

    pair = lax.all_gather(key_cache, "c", axis=0, tiled=True).reshape(2, *key_cache.shape)
    one, two = along_z(pair, 1), along_z(pair, 2)
    key_up = key_up.reshape(latent, heads * nope)
    value_up = value_up.transpose(1, 2, 0)
    place = jnp.concatenate([jnp.stack([y, z, c]).astype(jnp.int32), key_limit])
    half = h.astype(jnp.int32)[None]
    two, _, key_up, value_up, place, half = lax.optimization_barrier(
        (two, packed, key_up, value_up, place, half)
    )
    own = lax.dynamic_slice_in_dim(two, c, 1)
    three = along_z(two, 1)

    own, one, near_two = lax.optimization_barrier((own, one, two))
    four = along_z(own, 2)
    near = jnp.concatenate([one, near_two], axis=0)
    near_swapped = other_core(near)

    payload = swap_y(packed).reshape(4 * tokens, -1)
    queries, starts = latent_queries(query_start, payload, key_up, heads, nope, rope, 8)

    attend_part = functools.partial(
        attend, starts, place, queries, scale=scale, value_up=value_up
    )
    pairs = lambda steps: [(step, core) for step in steps for core in (0, 1)]
    partial = attend_part(
        keys=[pair, near, near_swapped], shards=pairs((0, 1, 2, -1, -2))
    )
    three, four, partial = lax.optimization_barrier((three, four, partial))
    partial = attend_part(
        keys=[three, other_core(three), four, other_core(four)],
        shards=pairs((3, -3)) + [(4, MINE), (4, OTHER)],
        before=partial,
    )
    values = merge(half, swap_y(partial.reshape(4, tokens, -1)), heads, 4)
    values, weight = lax.optimization_barrier((values, weight))
    weights = [weight, other_core(weight)]

    rows = swap_y(values)
    share = tokens // 8

    def summed(part):
        part = part.reshape(4 * tokens // 2, -1)
        product = jnp.concatenate(
            [
                lax.dot_general(
                    part, w, (((1,), (1,)), ((), ())), preferred_element_type=jnp.float32
                ).astype(jnp.bfloat16)
                for w in weights
            ],
            axis=1,
        )
        product = lax.all_to_all(
            product.reshape(16, share, -1), ("y", "x"), split_axis=0, concat_axis=0, tiled=True
        )
        return jnp.sum(product.reshape(4, 4, share, -1).astype(jnp.float32), axis=1)

    theirs = summed(rows[:, : tokens // 2]).astype(jnp.bfloat16)
    got = permute(theirs, ("h",), lambda at: {"h": 1 - at["h"]})
    mine = summed(rows[:, tokens // 2 :])
    return assemble(c.astype(jnp.int32)[None], mine, got, columns)


def solution(mesh):
    fine = Mesh(mesh.devices.reshape(tuple(SIZES.values())), NAMES)
    seq, head = ("y", "z", "c"), ("x", "h")
    in_specs = (
        P(seq, head, None),
        P(seq, head),
        P(None, seq),
        P(None, head, None),
        P(None, head, None),
        P(head, seq),
        P(),
        P(),
        P(seq),
    )
    return jax.shard_map(
        per_device, mesh=fine, in_specs=in_specs, out_specs=P(seq + head, None), check_vma=False
    )
```

```python
import functools
import math

import jax
import jax.numpy as jnp
import numpy as np
from jax import lax
from jax.experimental import pallas as pl
from jax.experimental.pallas import tpu as pltpu
from jax.sharding import Mesh, PartitionSpec as P

NEG = -1e30
LOG2E = 1.4426950408889634
SIZES = {"y": 4, "z": 8, "c": 2, "x": 4, "h": 2}
NAMES = tuple(SIZES)
STATS = 128
MINE, OTHER = 2, 3


def permute(x, names, move):
    dims = [SIZES[n] for n in names]
    pairs = []
    for place in np.ndindex(*dims):
        target = move(dict(zip(names, place)))
        pairs.append(
            (
                int(np.ravel_multi_index(place, dims)),
                int(np.ravel_multi_index([target[n] for n in names], dims)),
            )
        )
    return lax.ppermute(x, names, pairs)


def along_z(x, step):
    def move(at):
        place = (at["h"] * 8 + at["z"] + (step if at["c"] == 0 else -step)) % 16
        return {"z": place % 8, "c": at["c"], "h": place // 8}

    return permute(x, ("z", "c", "h"), move)


def other_core(x):
    return permute(x, ("c",), lambda at: {"c": 1 - at["c"]})


def swap_y(x):
    return lax.all_to_all(x, "y", split_axis=0, concat_axis=0, tiled=True)


def pack_kernel(order, content, rotary, out, *, block):
    left = content.shape[1]
    width = left + rotary.shape[1]
    row = lax.broadcasted_iota(jnp.int32, (out.shape[1], STATS), 0)
    number = jnp.where(row < block, order[0], order[1]).astype(jnp.float32).astype(out.dtype)
    for i in range(out.shape[0]):
        out[i, :, :left] = content[...]
        out[i, :, left:width] = rotary[...]
        out[i, :, width:] = number


def pack(order, content, rotary, block, copies):
    rows = content.shape[0]
    width = content.shape[1] + rotary.shape[1] + STATS
    vmem = pl.BlockSpec(memory_space=pltpu.VMEM)
    return pl.pallas_call(
        functools.partial(pack_kernel, block=block),
        in_specs=[pl.BlockSpec(memory_space=pltpu.SMEM), vmem, vmem],
        out_specs=vmem,
        out_shape=jax.ShapeDtypeStruct((copies, rows, width), jnp.bfloat16),
    )(order, content, rotary)


def query_kernel(start, payload, key_up, out, starts, *, heads, nope, rope):
    latent = key_up.shape[0]
    block = payload.shape[0] // starts.shape[0]
    for i in range(starts.shape[0]):
        number = payload[i * block : (i + 1) * block, payload.shape[1] - STATS :]
        starts[i] = start[0] + jnp.max(number.astype(jnp.float32)).astype(jnp.int32) * block
    for h in range(heads):
        cols = slice(h * nope, (h + 1) * nope)
        out[h, :latent, :] = lax.dot_general(
            key_up[:, cols],
            payload[:, cols],
            (((1,), (1,)), ((), ())),
            preferred_element_type=jnp.float32,
        ).astype(out.dtype)
    for p in range(heads // 2):
        cols = slice(heads * nope + 2 * p * rope, heads * nope + 2 * (p + 1) * rope)
        both = payload[:, cols].astype(jnp.float32).T.astype(out.dtype)
        out[2 * p, latent:, :] = both[:rope]
        out[2 * p + 1, latent:, :] = both[rope:]


def latent_queries(start, payload, key_up, heads, nope, rope, blocks):
    rows = payload.shape[0]
    latent = key_up.shape[0]
    smem, vmem = pl.BlockSpec(memory_space=pltpu.SMEM), pl.BlockSpec(memory_space=pltpu.VMEM)
    return pl.pallas_call(
        functools.partial(query_kernel, heads=heads, nope=nope, rope=rope),
        in_specs=[smem, vmem, vmem],
        out_specs=[vmem, smem],
        out_shape=[
            jax.ShapeDtypeStruct((heads, latent + rope, rows), jnp.bfloat16),
            jax.ShapeDtypeStruct((blocks,), jnp.int32),
        ],
        compiler_params=pltpu.CompilerParams(vmem_limit_bytes=48 * 1024 * 1024),
        cost_estimate=pl.CostEstimate(
            flops=2 * heads * rows * latent * nope, bytes_accessed=8 * 1024 * 1024, transcendentals=0
        ),
    )(start, payload, key_up)


def three_parts(x):
    parts = []
    for _ in range(3):
        part = x.astype(jnp.bfloat16).astype(jnp.float32)
        parts.append(part)
        x = x - part
    return parts


def read_stats(rows, heads):
    stats = rows[:, rows.shape[1] - STATS :].astype(jnp.float32)
    return stats[:, :heads] + stats[:, heads : 2 * heads] + stats[:, 2 * heads : 3 * heads]


def attend_kernel(
    starts, place, query, *rest, shards, coef, block, some, with_before
):
    *keys, value_up, before, out, turned, lses = rest
    heads, tokens = lses.shape
    value_dim, latent = value_up.shape[1:]
    width = keys[0].shape[2]
    tiles = [(r, i) for r in keys for i in range(r.shape[0])]
    columns = some * tokens
    limit = place[3]
    side = 1 - 2 * place[2]
    cores = {0: 0, 1: 1, MINE: place[2], OTHER: 1 - place[2]}
    bases = [
        ((place[0] * 8 + (place[1] + 8 - side * step) % 8) * 2 + cores[core]) * width
        for step, core in shards
    ]
    left = out.shape[1] - STATS

    for n, (r, i) in enumerate(tiles):
        turned[n * width : (n + 1) * width, :] = r[i].T
    if with_before:
        stats = before[:, left:].astype(jnp.float32).T
        olds = stats[:heads] + stats[heads : 2 * heads] + stats[2 * heads : 3 * heads]

    highest, nearest = bases[0], starts[0]
    for i in range(1, len(shards)):
        highest = jnp.maximum(highest, bases[i])
    for i in range(1, tokens // block):
        nearest = jnp.minimum(nearest, starts[i])
    sure = highest + width - 1 <= jnp.minimum(nearest, limit - 1)

    def run(masked, first):
        q = jnp.concatenate([query[first + i] for i in range(some)], axis=1)
        s = jnp.dot(turned[...], q, preferred_element_type=jnp.float32)
        if masked:
            token = lax.broadcasted_iota(jnp.int32, (1, columns), 1) % tokens
            last = token % block
            for i in range(tokens // block):
                last = last + jnp.where(token // block == i, starts[i], 0)
            last = jnp.minimum(last, limit - 1)
            row = lax.broadcasted_iota(jnp.int32, (width, columns), 0)
            s = jnp.concatenate(
                [
                    jnp.where(row + bases[n] <= last, s[n * width : (n + 1) * width], NEG)
                    for n in range(len(shards))
                ],
                axis=0,
            )
        top = jnp.max(s, axis=0, keepdims=True)
        if masked:
            top = jnp.maximum(top, NEG / 10)
        weights = jnp.exp2(s * coef - top * coef)
        total = jnp.sum(weights, axis=0, keepdims=True)
        k = jnp.concatenate([r[i, :latent] for r, i in tiles], axis=1)
        values = jnp.dot(k, weights.astype(jnp.bfloat16), preferred_element_type=jnp.float32)
        if masked:
            seen = total > 0
            total = jnp.where(seen, total, 1.0)
            lse = jnp.where(seen, top * coef + jnp.log2(total), NEG)
        else:
            lse = top * coef + jnp.log2(total)
        mixed = (values * (1.0 / total)).astype(jnp.bfloat16)
        mine = [lse[:, i * tokens : (i + 1) * tokens] for i in range(some)]
        new = [None] * some
        if with_before:
            old = []
            for i in range(some):
                past = olds[first + i : first + i + 1, :]
                peak = jnp.maximum(past, mine[i])
                a, b = jnp.exp2(past - peak), jnp.exp2(mine[i] - peak)
                old.append(a / (a + b))
                new[i] = b / (a + b)
                mine[i] = peak + jnp.log2(a + b)
            old = jnp.concatenate(old + [jnp.zeros((8 - some, tokens), jnp.float32)], axis=0).T
        for i in range(some):
            lses[first + i : first + i + 1, :] = mine[i]
            value = jnp.dot(
                value_up[first + i], mixed[:, i * tokens : (i + 1) * tokens], preferred_element_type=jnp.float32
            )
            if with_before:
                value = value * new[i]
            value = value.T
            cols = slice((first + i) * value_dim, (first + i + 1) * value_dim)
            if with_before:
                value = value + before[:, cols].astype(jnp.float32) * old[:, i : i + 1]
            out[:, cols] = value.astype(out.dtype)

    @pl.when(sure)
    def _():
        for first in range(0, heads, some):
            run(False, first)

    @pl.when(jnp.logical_not(sure))
    def _():
        for first in range(0, heads, some):
            run(True, first)

    empty = jnp.zeros((STATS - 3 * heads, tokens), jnp.float32)
    stats = jnp.concatenate(three_parts(lses[...]) + [empty], axis=0)
    out[:, left:] = stats.T.astype(out.dtype)


def attend(starts, place, query, keys, shards, value_up, scale, before=None, some=4):
    heads, depth, tokens = query.shape
    value_dim, latent = value_up.shape[1:]
    width = keys[0].shape[2]
    kernel = functools.partial(
        attend_kernel,
        shards=shards,
        coef=scale * LOG2E,
        block=tokens // starts.shape[0],
        some=some,
        with_before=before is not None,
    )
    if before is None:
        before = jnp.zeros((16, STATS), jnp.bfloat16)
    return pl.pallas_call(
        kernel,
        in_specs=[pl.BlockSpec(memory_space=pltpu.SMEM)] * 2
        + [pl.BlockSpec(memory_space=pltpu.VMEM)] * (len(keys) + 3),
        out_specs=pl.BlockSpec(memory_space=pltpu.VMEM),
        scratch_shapes=[
            pltpu.VMEM((len(shards) * width, depth), jnp.bfloat16),
            pltpu.VMEM((heads, tokens), jnp.float32),
        ],
        out_shape=jax.ShapeDtypeStruct((tokens, heads * value_dim + STATS), jnp.bfloat16),
        compiler_params=pltpu.CompilerParams(vmem_limit_bytes=40 * 1024 * 1024),
    )(starts, place, query, *keys, value_up, before)


def merge_kernel(half, parts, out, *, heads, sources):
    width = out.shape[2]
    share = out.shape[1] // 8
    first = lambda value, which: [
        value[i * share : (i + 1) * share] for i in range(8) if i % 2 == which
    ]
    each = width // heads
    lses = [read_stats(parts.at[s], heads) for s in range(sources)]
    top = functools.reduce(jnp.maximum, lses)
    weights = [jnp.exp2(v - top) for v in lses]
    total = functools.reduce(jnp.add, weights)
    weights = [w / total for w in weights]
    for h in range(heads):
        cols = slice(h * each, (h + 1) * each)
        value = functools.reduce(
            jnp.add,
            [
                weights[s][:, h : h + 1] * parts[s, :, cols].astype(jnp.float32)
                for s in range(sources)
            ],
        )
        even, odd = first(value, 0), first(value, 1)
        value = jnp.where(
            half[0] == 0, jnp.concatenate(odd + even, axis=0), jnp.concatenate(even + odd, axis=0)
        ).astype(out.dtype)
        for i in range(out.shape[0]):
            out[i, :, cols] = value


def merge(half, parts, heads, copies):
    sources, tokens, width = parts.shape
    return pl.pallas_call(
        functools.partial(merge_kernel, heads=heads, sources=sources),
        in_specs=[
            pl.BlockSpec(memory_space=pltpu.SMEM),
            pl.BlockSpec(memory_space=pltpu.VMEM),
        ],
        out_shape=jax.ShapeDtypeStruct((copies, tokens, width - STATS), jnp.bfloat16),
    )(half, parts)


def per_device(
    query_content,
    query_rotary,
    key_cache,
    key_up,
    value_up,
    output_weight,
    query_start,
    key_limit,
    block_order,
):
    tokens, heads, nope = query_content.shape
    latent = key_up.shape[0]
    rope = query_rotary.shape[1] // heads
    columns = output_weight.shape[1]
    block = tokens // 2
    scale = 1.0 / math.sqrt(nope + rope)
    y, z, c, h = (lax.axis_index(n) for n in ("y", "z", "c", "h"))

    weight = lax.all_gather(output_weight.T, "z", axis=0, tiled=True)

    content = query_content.reshape(tokens, heads * nope)
    packed = pack(block_order, content, query_rotary, block, 4)

    pair = lax.all_gather(key_cache, "c", axis=0, tiled=True).reshape(2, *key_cache.shape)
    one, two = along_z(pair, 1), along_z(pair, 2)
    key_up = key_up.reshape(latent, heads * nope)
    value_up = value_up.transpose(1, 2, 0)
    place = jnp.concatenate([jnp.stack([y, z, c]).astype(jnp.int32), key_limit])
    half = h.astype(jnp.int32)[None]
    two, _, key_up, value_up, place, half = lax.optimization_barrier(
        (two, packed, key_up, value_up, place, half)
    )
    own = lax.dynamic_slice_in_dim(two, c, 1)
    three = along_z(two, 1)
    own, one, near_two = lax.optimization_barrier((own, one, two))
    four = along_z(own, 2)
    near = jnp.concatenate([one, near_two], axis=0)
    near_swapped = other_core(near)

    payload = swap_y(packed).reshape(4 * tokens, -1)
    queries, starts = latent_queries(query_start, payload, key_up, heads, nope, rope, 8)

    attend_part = functools.partial(
        attend, starts, place, queries, scale=scale, value_up=value_up
    )
    pairs = lambda steps: [(step, core) for step in steps for core in (0, 1)]
    partial = attend_part(
        keys=[pair, near, near_swapped], shards=pairs((0, 1, 2, -1, -2))
    )
    three, four, partial = lax.optimization_barrier((three, four, partial))
    partial = attend_part(
        keys=[three, other_core(three), four, other_core(four)],
        shards=pairs((3, -3)) + [(4, MINE), (4, OTHER)],
        before=partial,
    )
    values = merge(half, swap_y(partial.reshape(4, tokens, -1)), heads, 4)
    values, weight = lax.optimization_barrier((values, weight))
    weights = [weight, other_core(weight)]

    rows = swap_y(values)
    share = tokens // 8

    def summed(part):
        part = part.reshape(4 * tokens // 2, -1)
        product = jnp.concatenate(
            [
                lax.dot_general(
                    part, w, (((1,), (1,)), ((), ())), preferred_element_type=jnp.float32
                ).astype(jnp.bfloat16)
                for w in weights
            ],
            axis=1,
        )
        product = lax.all_to_all(
            product.reshape(16, share, -1), ("y", "x"), split_axis=0, concat_axis=0, tiled=True
        )
        return jnp.sum(product.reshape(4, 4, share, -1).astype(jnp.float32), axis=1)

    theirs = summed(rows[:, : tokens // 2]).astype(jnp.bfloat16)
    got = permute(theirs, ("h",), lambda at: {"h": 1 - at["h"]})
    mine = summed(rows[:, tokens // 2 :])
    total = (mine + got.astype(jnp.float32)).astype(jnp.bfloat16)
    total = total.reshape(4, share, 2, 8, columns)
    total = jnp.where(c == 0, total, total[:, :, ::-1])
    return total.transpose(1, 0, 3, 2, 4).reshape(share, 16 * 4 * columns)


def solution(mesh):
    fine = Mesh(mesh.devices.reshape(tuple(SIZES.values())), NAMES)
    seq, head = ("y", "z", "c"), ("x", "h")
    in_specs = (
        P(seq, head, None),
        P(seq, head),
        P(None, seq),
        P(None, head, None),
        P(None, head, None),
        P(head, seq),
        P(),
        P(),
        P(seq),
    )
    return jax.shard_map(
        per_device, mesh=fine, in_specs=in_specs, out_specs=P(seq + head, None), check_vma=False
    )
```
